128 devices in a mesh: node: 64 (over z, y_lo, x, core), head: 2 (over y_hi).
Axes of the slice: x: 4, y: 4 (y_hi: 2, y_lo: 2; y = y_hi * 2 + y_lo), z: 4, core: 2. Of those that a mesh axis runs over, the one named last changes fastest.
Arguments:
- features: bfloat16 [8192, 1024], P('node', 'head'), may hold values from -6 to 6
- queries: bfloat16 [8192, 1024], P('node', 'head'), may hold values from -6 to 6
- keys: bfloat16 [8192, 1024], P('node', 'head'), may hold values from -6 to 6
- values: bfloat16 [8192, 1024], P('node', 'head'), may hold values from -6 to 6
- attn_mix: bfloat16 [8192, 1024], P('node', 'head'), may hold values from -6 to 6
- log_sums: float32 [16, 8192], P('head', 'node'), as said below
- out_weight: bfloat16 [1024, 1024], P('head'), may hold values from -0.1875 to 0.1875
- msg_weight: bfloat16 [1024, 1024], P('head'), may hold values from -0.1875 to 0.1875
- edge_tiles: bfloat16 [64, 8, 128, 128], P('node'), may hold values from -0.25 to 0.25
- edge_source: int32 [64, 8], P('node'), may hold values from 0 to 63, as said below
- edge_count: int32 [64], P('node'), may hold values from 1 to 8, as said below
- out_grad: bfloat16 [8192, 1024], P('node', 'head'), may hold values from -6 to 6
Outputs:
- grad_features: bfloat16 [8192, 1024], P('node', 'head')
- grad_queries: bfloat16 [8192, 1024], P('node', 'head')
- grad_keys: bfloat16 [8192, 1024], P('node', 'head')
- grad_values: bfloat16 [8192, 1024], P('node', 'head')
- out_weight_grad: float32 [1024, 1024], P('head')
- msg_weight_grad: float32 [1024, 1024], P('head')
The draws below stay inside these ranges and needn't reach their ends.
Inputs may be any that keep to these rules, and one draw needn't show every extreme that they name: `log_sums`: the saved statistic of each row, of the size of the log of 8192. The partition of edge_source[b, e] lies at most 3 partitions before or after the partition of b, counted cyclically over the partitions; some slot lies exactly 3 partitions after and some exactly 3 before; slots that are not live hold valid block numbers too. `edge_count`: some block has all 8 slots live.
All inputs are finite; a program needn't handle non-finite values.
Results may differ from the reference program's by a relative error of at most 0.012.
Values may be sent and summed in bfloat16 or wider, within the bound.
No kernel may reach another device: no remote copies, remote signals or barrier semaphores. Data moves between devices by JAX's collectives and lax.ppermute only.
A program may use at most 256 MiB of HBM per device.

```python
import math
import jax
import jax.numpy as jnp
from jax import lax

D = 1024
HEADS = 16
HEAD_DIM = 64
NODE_DEV = 128
BLOCK = 128
EMAX = 8
REACH = 3
NODES = 8192
BLOCKS = 64
N_NODE = 64


def draw_log_sums(key, part):
    key = jax.random.fold_in(key, 11)
    centre = math.log(NODES) + 0.5
    jitter = jax.random.uniform(key, (HEADS, NODES), jnp.float32, -0.6, 0.6)
    return (centre + jitter).astype(jnp.float32)


def draw_edge_count(key, part):
    key = jax.random.fold_in(key, 12)
    first, second, third = jax.random.split(key, 3)
    heavy = jax.random.randint(first, (BLOCKS,), 0, 4) == 0
    light = jax.random.randint(second, (BLOCKS,), 1, EMAX // 2 + 1)
    count = jnp.where(heavy, EMAX, light)
    chosen = jax.random.randint(third, (), 0, BLOCKS)
    count = count.at[chosen].set(EMAX)
    return count.astype(jnp.int32)


def draw_edge_source(key, part):
    key = jax.random.fold_in(key, 13)
    first, second = jax.random.split(key, 2)
    per_part = NODE_DEV // BLOCK
    parts = NODES // NODE_DEV
    offset = jax.random.randint(first, (BLOCKS, EMAX), -REACH, REACH + 1)
    offset = offset.at[0, 0].set(REACH)
    offset = offset.at[BLOCKS - 1, 0].set(-REACH)
    inner = jax.random.randint(second, (BLOCKS, EMAX), 0, per_part)
    home = jnp.arange(BLOCKS, dtype=jnp.int32) // per_part
    source = (home[:, None] + offset) % parts * per_part + inner
    return source.astype(jnp.int32)


def block_scale(key, shape, cuts, smallest, top_value):
    factor_of = 1.0
    for dim, shards_of in cuts:
        steps = jax.random.uniform(jax.random.fold_in(jax.random.fold_in(key, 6), dim), (shards_of,), jnp.float32, smallest / len(cuts), top_value / len(cuts))
        factor_of = factor_of * jnp.repeat(jnp.exp(steps), shape[dim] // shards_of).reshape((-1,) + (1,) * (len(shape) - 1 - dim))
    return factor_of


def normal_values(stream_key, shape, width, bound, pieces=(), held_as=jnp.bfloat16):
    loudness = block_scale(stream_key, shape, pieces, -0.22, 0.18) if pieces else 1.0
    entries = jax.random.normal(stream_key, shape, jnp.float32) * width * loudness
    return jnp.minimum(jnp.maximum(entries, -bound), bound).astype(held_as)


def setup_inputs(seed: int = 0) -> dict:
    streams_of = jax.random.split(jax.random.key(seed), 13)
    features = normal_values(streams_of[0], (NODES, D), 1.0, 6.0, ((0, 64), (1, 2)))
    queries = normal_values(streams_of[1], (NODES, D), 1.0, 6.0, ((0, 64), (1, 2)))
    keys = normal_values(streams_of[2], (NODES, D), 1.0, 6.0, ((0, 64), (1, 2)))
    values = normal_values(streams_of[3], (NODES, D), 1.0, 6.0, ((0, 64), (1, 2)))
    attn_mix = normal_values(streams_of[4], (NODES, D), 1.0, 6.0, ((0, 64), (1, 2)))
    log_sums = draw_log_sums(jax.random.fold_in(streams_of[12], 71), 0)
    out_weight = normal_values(streams_of[6], (D, D), D ** -0.5, 0.1875, ((0, 2),))
    msg_weight = normal_values(streams_of[7], (D, D), D ** -0.5, 0.1875, ((0, 2),))
    edge_tiles = normal_values(streams_of[8], (BLOCKS, EMAX, BLOCK, BLOCK), (BLOCK * 4) ** -0.5, 0.25, ((0, 64),))
    edge_source = draw_edge_source(jax.random.fold_in(streams_of[12], 71), 0)
    edge_count = draw_edge_count(jax.random.fold_in(streams_of[12], 71), 0)
    out_grad = normal_values(streams_of[11], (NODES, D), 1.0, 6.0, ((0, 64), (1, 2)))
    return {"features": features, "queries": queries, "keys": keys, "values": values, "attn_mix": attn_mix, "log_sums": log_sums, "out_weight": out_weight, "msg_weight": msg_weight, "edge_tiles": edge_tiles, "edge_source": edge_source, "edge_count": edge_count, "out_grad": out_grad}


def attention_head(operands):
    query, key_rows, value_rows, grad_rows, log_row, spread_row = operands
    scale = 1.0 / math.sqrt(HEAD_DIM)
    scores = jnp.dot(query, key_rows.T, preferred_element_type=jnp.float32) * scale
    softmax_rows = jnp.exp(scores - log_row[:, None])
    grad_scores = jnp.dot(grad_rows, value_rows.T, preferred_element_type=jnp.float32)
    score_grad = (softmax_rows * (grad_scores - spread_row[:, None])).astype(jnp.bfloat16)
    softmax_low = softmax_rows.astype(jnp.bfloat16)
    grad_value = jnp.dot(softmax_low.T, grad_rows, preferred_element_type=jnp.float32)
    grad_query = jnp.dot(score_grad, key_rows, preferred_element_type=jnp.float32) * scale
    grad_key = jnp.dot(score_grad.T, query, preferred_element_type=jnp.float32) * scale
    return (grad_query.astype(jnp.bfloat16), grad_key.astype(jnp.bfloat16), grad_value.astype(jnp.bfloat16))

def by_head(array):
    return array.reshape(NODES, HEADS, HEAD_DIM).transpose(1, 0, 2)

def from_heads(array):
    return array.transpose(1, 0, 2).reshape(NODES, D)

def reference(features, queries, keys, values, attn_mix, log_sums, out_weight, msg_weight, edge_tiles, edge_source, edge_count, out_grad):
    grad_mix = jnp.dot(out_grad, out_weight.T, preferred_element_type=jnp.float32).astype(jnp.bfloat16)
    grad_aggregate = jnp.dot(out_grad, msg_weight.T, preferred_element_type=jnp.float32).astype(jnp.bfloat16)
    live = jnp.arange(EMAX, dtype=jnp.int32)[None, :] < edge_count[:, None]
    tiles = jnp.where(live[:, :, None, None], edge_tiles, jnp.zeros((), jnp.bfloat16))
    blocks = features.reshape(BLOCKS, BLOCK, D)
    picked = blocks[edge_source]
    aggregate = jnp.einsum('beij,bejd->bid', tiles.astype(jnp.float32), picked.astype(jnp.float32))
    aggregate = aggregate.reshape(NODES, D).astype(jnp.bfloat16)
    out_weight_grad = jnp.dot(attn_mix.T, out_grad, preferred_element_type=jnp.float32)
    msg_weight_grad = jnp.dot(aggregate.T, out_grad, preferred_element_type=jnp.float32)
    spread = lax.optimization_barrier(jnp.sum((grad_mix.astype(jnp.float32) * attn_mix.astype(jnp.float32)).reshape(NODES, HEADS, HEAD_DIM), axis=2)).T
    grad_query, grad_key, grad_value = lax.map(attention_head, (by_head(queries), by_head(keys), by_head(values), by_head(grad_mix), log_sums, spread))
    parts = N_NODE
    per_part = NODE_DEV // BLOCK
    home = jnp.arange(BLOCKS, dtype=jnp.int32) // per_part
    distance = (edge_source // per_part - home[:, None]) % parts
    distance = jnp.where(distance > REACH, distance - parts, distance)
    slot_table = jax.nn.one_hot(edge_source % per_part, per_part, dtype=jnp.float32)
    grad_blocks = grad_aggregate.reshape(BLOCKS, BLOCK, D).astype(jnp.float32)
    tiles_wide = tiles.astype(jnp.float32)
    total = jnp.zeros((parts, NODE_DEV, D), jnp.float32)
    for offset in range(-REACH, REACH + 1):
        weights = slot_table * (distance == offset)[:, :, None].astype(jnp.float32)
        moved = jnp.einsum('bek,beij,bid->bkjd', weights, tiles_wide, grad_blocks)
        moved = moved.reshape(parts, per_part, per_part, BLOCK, D).sum(axis=1).reshape(parts, NODE_DEV, D)
        rounded = lax.optimization_barrier(moved.astype(jnp.bfloat16))
        total = total + jnp.roll(rounded, offset, axis=0).astype(jnp.float32)
    grad_features = total.reshape(NODES, D).astype(jnp.bfloat16)
    return (grad_features, from_heads(grad_query), from_heads(grad_key), from_heads(grad_value), out_weight_grad, msg_weight_grad)
```

```python
import functools
import math

import jax
import jax.numpy as jnp
from jax import lax
from jax.experimental import pallas as pl
from jax.experimental.pallas import tpu as pltpu
from jax.sharding import Mesh
from jax.sharding import PartitionSpec as P

BLOCK = 128
REACH = 3
LANES = 128
PAIRS = 4
STAT = 16
NODE = ("z", "y", "x", "c")
BF16 = jnp.bfloat16
F32 = jnp.float32
VMEM_LIMIT = 48 * 1024 * 1024

NT = (((1,), (1,)), ((), ()))
NN = (((1,), (0,)), ((), ()))
TN = (((0,), (0,)), ((), ()))


def dot(a, b, dims):
    return lax.dot_general(a, b, dims, preferred_element_type=F32)


def shift(value, axis, steps):
    count = lax.axis_size(axis)
    return lax.ppermute(value, axis, [(i, (i + steps) % count) for i in range(count)])


def swap(value, axes, mask):
    count = lax.axis_size(axes)
    return lax.ppermute(value, axes, [(i, i ^ mask) for i in range(count)])


def place_in_group():
    return lax.axis_index("y") * 2 + lax.axis_index("c")


def call(kernel, outs, *args, scratch=(), smem=0, flops=0, name=None):
    specs = [pl.BlockSpec(memory_space=pltpu.SMEM)] * smem
    specs += [pl.BlockSpec(memory_space=pltpu.VMEM)] * (len(args) - smem)
    size = sum(math.prod(a.shape) * a.dtype.itemsize for a in (*args, *outs))
    return pl.pallas_call(
        kernel,
        out_shape=outs,
        in_specs=specs,
        out_specs=[pl.BlockSpec(memory_space=pltpu.VMEM)] * len(outs),
        scratch_shapes=list(scratch),
        cost_estimate=pl.CostEstimate(flops=flops, bytes_accessed=size, transcendentals=0),
        compiler_params=pltpu.CompilerParams(vmem_limit_bytes=VMEM_LIMIT),
        name=name,
    )(*args)


def shaped(shape, dtype=BF16):
    return jax.ShapeDtypeStruct(shape, dtype)


def three_pieces(value):
    high = value.astype(BF16)
    rest = value - high.astype(F32)
    middle = rest.astype(BF16)
    low = (rest - middle.astype(F32)).astype(BF16)
    return jnp.concatenate(
        [high.astype(F32), middle.astype(F32), low.astype(F32), jnp.zeros((STAT - 6, LANES), F32)],
        axis=0,
    ).astype(BF16)


def pair_rows(table, pair):
    rows = table[0:2]
    for other in range(1, PAIRS):
        rows = jnp.where(pair == other, table[2 * other : 2 * other + 2], rows)
    return rows


def outgoing_kernel(q_ref, k_ref, v_ref, log_ref, *pay_refs):
    me = place_in_group()
    logs = log_ref[...]
    for j, pay in enumerate(pay_refs):
        pair = me ^ j
        columns = pl.ds(pl.multiple_of(pair * LANES, LANES), LANES)
        pay[0:128] = q_ref[:, columns]
        pay[128:144] = three_pieces(pair_rows(logs, pair))
        pay[144:272] = k_ref[:, columns]
        pay[272:400] = v_ref[:, columns]


def join_kernel(*refs):
    q_out, kv_out = refs[4:]
    for j, pay in enumerate(refs[:4]):
        q_out[j * 144 : (j + 1) * 144] = pay[0:144]
        kv_out[j * 256 : (j + 1) * 256] = pay[144:400]


def mix_kernel(own_ref, other_ref, weight_ref, mix_ref, *pay_refs):
    side = lax.axis_index("h")
    half = own_ref.shape[1]
    own_columns = pl.ds(pl.multiple_of(side * half, half), half)
    other_columns = pl.ds(pl.multiple_of((1 - side) * half, half), half)
    grad = dot(own_ref[...], weight_ref[:, own_columns], NT)
    grad = (grad + dot(other_ref[...], weight_ref[:, other_columns], NT)).astype(BF16)
    product = grad.astype(F32) * mix_ref[...].astype(F32)
    turned = product.T
    rows = [jnp.sum(turned[64 * i : 64 * (i + 1)], axis=0, keepdims=True) for i in range(8)]
    spread = jnp.concatenate(rows, axis=0)
    me = place_in_group()
    for j, pay in enumerate(pay_refs):
        pair = me ^ j
        block = grad[:, 0:LANES]
        for other in range(1, PAIRS):
            block = jnp.where(pair == other, grad[:, other * LANES : (other + 1) * LANES], block)
        pay[0:128] = block
        pay[128:144] = three_pieces(pair_rows(spread, pair))


def join_grad_kernel(*refs):
    for j, pay in enumerate(refs[:4]):
        refs[4][j * 144 : (j + 1) * 144] = pay[...]


TILE = 512


def attention_kernel(*refs):
    q_in, do_in, kv_in = refs[0:4], refs[4:8], refs[8:12]
    dq_out, dkv_out = refs[12:16], refs[16:20]
    keys, values, keys_t, query, grad, logs, spread, dq, dk, dv = refs[20:]
    lane = lax.broadcasted_iota(jnp.int32, (128, LANES), 1)
    for k in range(4):
        for j in range(4):
            rows = slice((k * 4 + j) * 128, (k * 4 + j + 1) * 128)
            block = kv_in[k][j * 256 : j * 256 + 128]
            keys[rows] = block
            keys_t[:, rows] = block.astype(F32).T.astype(BF16)
            values[rows] = kv_in[k][j * 256 + 128 : (j + 1) * 256]
            for source, table, stat, factor in (
                (q_in[k], query, logs, 0.125),
                (do_in[k], grad, spread, 1.0),
            ):
                block = source[j * 144 : j * 144 + 128].astype(F32) * factor
                table[0, rows] = jnp.where(lane < 64, block, 0.0).astype(BF16)
                table[1, rows] = jnp.where(lane < 64, 0.0, block).astype(BF16)
                pieces = source[j * 144 + 128 : (j + 1) * 144].astype(F32)
                stat[:, rows] = pieces[0:2] + pieces[2:4] + pieces[4:6]
    dq[...] = jnp.zeros_like(dq)
    steps = keys.shape[0] // TILE

    @pl.loop(0, steps)
    def _(kb):
        krows = pl.ds(pl.multiple_of(kb * TILE, TILE), TILE)
        dk[krows] = jnp.zeros((TILE, LANES), F32)
        dv[krows] = jnp.zeros((TILE, LANES), F32)
        key_tile, value_tile = keys[krows], values[krows]

        @pl.loop(0, steps)
        def _(qb):
            qrows = pl.ds(pl.multiple_of(qb * TILE, TILE), TILE)
            for h in range(2):
                query_tile, grad_tile = query[h, qrows], grad[h, qrows]
                scores = dot(key_tile, query_tile, NT) - logs[h : h + 1, qrows]
                soft = jnp.exp(scores)
                change = dot(value_tile, grad_tile, NT) - spread[h : h + 1, qrows]
                score_grad = (soft * change).astype(BF16)
                dv[krows] += dot(soft.astype(BF16), grad_tile, NN)
                dk[krows] += dot(score_grad, query_tile, NN)
                head = slice(64 * h, 64 * (h + 1))
                dq[head, qrows] += dot(keys_t[head, krows], score_grad, NN)

    for k in range(4):
        for j in range(4):
            rows = slice((k * 4 + j) * 128, (k * 4 + j + 1) * 128)
            dq_out[k][j * 128 : (j + 1) * 128] = (dq[:, rows].T * 0.125).astype(BF16)
            dkv_out[k][j * 256 : j * 256 + 128] = dk[rows].astype(BF16)
            dkv_out[k][j * 256 + 128 : (j + 1) * 256] = dv[rows].astype(BF16)


def sum_kernel(*refs):
    dq = [r[...].astype(F32) for r in refs[0:4]]
    dkv = [r[...].astype(F32) for r in refs[4:8]]
    dq = (dq[0] + dq[1] + dq[2] + dq[3]).astype(BF16)
    dkv = (dkv[0] + dkv[1] + dkv[2] + dkv[3]).astype(BF16)
    for j, pay in enumerate(refs[8:12]):
        pay[0:128] = dq[j * 128 : (j + 1) * 128]
        pay[128:384] = dkv[j * 256 : (j + 1) * 256]


def place_kernel(*refs):
    me = place_in_group()
    dq, dk, dv = refs[4:]
    for j, pay in enumerate(refs[:4]):
        columns = pl.ds(pl.multiple_of((me ^ j) * LANES, LANES), LANES)
        dq[:, columns] = pay[0:128]
        dk[:, columns] = pay[128:256]
        dv[:, columns] = pay[256:384]


def share_kernel(source_ref, count_ref, tiles_ref, grad_ref, *refs):
    outs, total = refs[:-1], refs[-1]
    window = 2 * REACH + 1
    parts = lax.axis_size(NODE)
    home = lax.axis_index(NODE)
    total[...] = jnp.zeros_like(total)
    grad = grad_ref[...]
    for e in range(tiles_ref.shape[1]):

        @pl.when(e < count_ref[0])
        def _():
            distance = lax.rem(source_ref[0, e] - home + REACH + 2 * parts, parts)
            slot = jnp.clip(distance, 0, window - 1)
            total[slot] += dot(tiles_ref[0, e], grad, TN)

    for o, out in enumerate(outs):
        out[...] = total[o].astype(out.dtype)


def weights_kernel(own_ref, other_ref, g_own_ref, g_other_ref, mix_ref, feat_ref, weight_ref, gf_ref, keep_ref, send_ref):
    side = lax.axis_index("h")
    core = lax.axis_index("c")
    half = own_ref.shape[1]
    own_columns = pl.ds(pl.multiple_of(side * half, half), half)
    other_columns = pl.ds(pl.multiple_of((1 - side) * half, half), half)
    features = dot(g_own_ref[...], weight_ref[:, own_columns], NT)
    features = features + dot(g_other_ref[...], weight_ref[:, other_columns], NT)
    gf_ref[...] = features.astype(BF16)
    mix = mix_ref[...].astype(F32).T.astype(BF16)
    feat = feat_ref[...].astype(F32).T.astype(BF16)

    def put(out_refs):
        for left, rights, out in zip((mix, feat), ((own_ref, other_ref), (g_own_ref, g_other_ref)), out_refs):
            out[:, own_columns] = dot(left, rights[0][...], NN).astype(BF16)
            out[:, other_columns] = dot(left, rights[1][...], NN).astype(BF16)

    @pl.when(core == 0)
    def _():
        put((keep_ref, send_ref))

    @pl.when(core == 1)
    def _():
        put((send_ref, keep_ref))


def scatter_kernel(axis, received, *refs):
    me = lax.axis_index(axis)
    outs = refs[received:]
    count = len(outs)
    rows = outs[0].shape[0]
    for k, out in enumerate(outs):
        at = pl.ds(pl.multiple_of(lax.rem(me + k, count) * rows, rows), rows)
        total = refs[0][at].astype(F32)
        for ref in refs[1:received]:
            total = total + ref[at].astype(F32)
        out[...] = total.astype(BF16)


def gather_kernel(axis, *refs):
    me = lax.axis_index(axis)
    out = refs[-1]
    count = len(refs) - 1
    rows = refs[0].shape[0]
    for k in range(count):
        at = pl.ds(pl.multiple_of(lax.rem(me - k + count, count) * rows, rows), rows)
        out[at] = refs[k][...]


def final_kernel(own_ref, other_ref, first_ref, second_ref):
    core = lax.axis_index("c")

    @pl.when(core == 0)
    def _():
        first_ref[...] = own_ref[...].astype(F32)
        second_ref[...] = other_ref[...].astype(F32)

    @pl.when(core == 1)
    def _():
        first_ref[...] = other_ref[...].astype(F32)
        second_ref[...] = own_ref[...].astype(F32)


def reduce_weights(keep, send):
    rows, columns = keep.shape
    parts = [keep, swap(send, "c", 1)]
    for axis, count in (("x", 4), ("z", 4), ("y", 2)):
        rows = rows // count
        blocks = call(
            functools.partial(scatter_kernel, axis, len(parts)),
            [shaped((rows, columns))] * count,
            *parts,
            name="scatter_" + axis,
        )
        parts = [blocks[0]] + [shift(blocks[k], axis, k) for k in range(1, count)]
    whole = (parts[0].astype(F32) + parts[1].astype(F32)).astype(BF16)
    for axis, count in (("y", 2), ("z", 4), ("x", 4)):
        blocks = [whole] + [shift(whole, axis, k) for k in range(1, count)]
        rows = rows * count
        (whole,) = call(
            functools.partial(gather_kernel, axis),
            [shaped((rows, columns))],
            *blocks,
            name="gather_" + axis,
        )
    other = swap(whole, "c", 1)
    return call(final_kernel, [shaped(whole.shape, F32)] * 2, whole, other, name="final")


def body(
    features,
    queries,
    keys,
    values,
    attn_mix,
    log_sums,
    out_weight,
    msg_weight,
    edge_tiles,
    edge_source,
    edge_count,
    out_grad,
):
    rows, columns = out_grad.shape
    other_grad = swap(out_grad, "h", 1)
    pays = call(
        outgoing_kernel, [shaped((400, LANES))] * 4, queries, keys, values, log_sums, name="outgoing"
    )
    pays = [pays[0]] + [swap(pays[j], ("y", "c"), j) for j in range(1, 4)]
    near_q, near_kv = call(
        join_kernel, [shaped((576, LANES)), shaped((1024, LANES))], *pays, name="join"
    )
    all_kv = [near_kv] + [shift(near_kv, "x", k) for k in range(1, 4)]
    all_q = [near_q] + [shift(near_q, "z", k) for k in range(1, 4)]

    pays = call(
        mix_kernel,
        [shaped((144, LANES))] * 4,
        out_grad,
        other_grad,
        out_weight,
        attn_mix,
        name="mix",
    )
    pays = [pays[0]] + [swap(pays[j], ("y", "c"), j) for j in range(1, 4)]
    (near_do,) = call(join_grad_kernel, [shaped((576, LANES))], *pays, name="join_grad")
    all_do = [near_do] + [shift(near_do, "z", k) for k in range(1, 4)]

    shares = call(
        share_kernel,
        [shaped((rows, columns), F32 if o == REACH else BF16) for o in range(2 * REACH + 1)],
        edge_source,
        edge_count,
        edge_tiles,
        out_grad,
        smem=2,
        scratch=[pltpu.VMEM((2 * REACH + 1, rows, columns), F32)],
        name="shares",
    )
    total = shares[REACH]
    for o in range(2 * REACH + 1):
        if o != REACH:
            total = total + shift(shares[o], NODE, o - REACH).astype(F32)
    near_g = total.astype(BF16)
    other_g = swap(near_g, "h", 1)
    grad_features, keep, send = call(
        weights_kernel,
        [shaped((rows, columns)), shaped((columns, 2 * columns)), shaped((columns, 2 * columns))],
        out_grad,
        other_grad,
        near_g,
        other_g,
        attn_mix,
        features,
        msg_weight,
        name="weights",
    )
    out_weight_grad, msg_weight_grad = reduce_weights(keep, send)

    big = 2048
    results = call(
        attention_kernel,
        [shaped((512, LANES))] * 4 + [shaped((1024, LANES))] * 4,
        *all_q,
        *all_do,
        *all_kv,
        scratch=[
            pltpu.VMEM((big, LANES), BF16),
            pltpu.VMEM((big, LANES), BF16),
            pltpu.VMEM((LANES, big), BF16),
            pltpu.VMEM((2, big, LANES), BF16),
            pltpu.VMEM((2, big, LANES), BF16),
            pltpu.VMEM((2, big), F32),
            pltpu.VMEM((2, big), F32),
            pltpu.VMEM((LANES, big), F32),
            pltpu.VMEM((big, LANES), F32),
            pltpu.VMEM((big, LANES), F32),
        ],
        flops=8 * 10 * big * big * 64,
        name="attention",
    )
    parts = [results[0]] + [shift(results[k], "z", -k) for k in range(1, 4)]
    parts += [results[4]] + [shift(results[4 + k], "x", -k) for k in range(1, 4)]
    pays = call(sum_kernel, [shaped((384, LANES))] * 4, *parts, name="sum")
    pays = [pays[0]] + [swap(pays[j], ("y", "c"), j) for j in range(1, 4)]
    grad_query, grad_key, grad_value = call(
        place_kernel, [shaped((rows, columns))] * 3, *pays, name="place"
    )
    return (grad_features, grad_query, grad_key, grad_value, out_weight_grad, msg_weight_grad)


def solution(mesh):
    fine = Mesh(mesh.devices.reshape(4, 2, 4, 2, 2), NODE + ("h",))
    both = P(NODE, "h")
    placed = (
        both,
        both,
        both,
        both,
        both,
        P("h", NODE),
        P("h", None),
        P("h", None),
        P(NODE, None, None, None),
        P(NODE, None),
        P(NODE),
        both,
    )
    return jax.shard_map(
        body,
        mesh=fine,
        in_specs=placed,
        out_specs=(both, both, both, both, P("h", None), P("h", None)),
        check_vma=False,
    )
```

```python
import functools
import math

import jax
import jax.numpy as jnp
from jax import lax
from jax.experimental import pallas as pl
from jax.experimental.pallas import tpu as pltpu
from jax.sharding import Mesh
from jax.sharding import PartitionSpec as P

BLOCK = 128
REACH = 3
LANES = 128
PAIRS = 4
STAT = 16
GROUP = 512
NODE = ("z", "y", "x", "c")
BF16 = jnp.bfloat16
F32 = jnp.float32
VMEM_LIMIT = 48 * 1024 * 1024

NT = (((1,), (1,)), ((), ()))
NN = (((1,), (0,)), ((), ()))
TN = (((0,), (0,)), ((), ()))


def dot(a, b, dims):
    return lax.dot_general(a, b, dims, preferred_element_type=F32)


def swap(value, axes, mask):
    count = lax.axis_size(axes)
    return lax.ppermute(value, axes, [(i, i ^ mask) for i in range(count)])


NEXT = ((1, 0, 3, 2), (3, 2, 1, 0))


def meet(value, axis, step):
    pairs = [
        (2 * i + core, 2 * NEXT[(step + core) % 2][i] + core) for i in range(4) for core in range(2)
    ]
    return lax.ppermute(value, (axis, "c"), pairs)


def side_at(axis, step):
    place, core = lax.axis_index(axis), lax.axis_index("c")
    first = jnp.where((place == 1) | (place == 2), 1, 0)
    second = jnp.where(place >= 2, 1, 0)
    return jnp.where(core == step, first, second)


def place_in_group():
    return lax.axis_index("y") * 2 + lax.axis_index("c")


class Order:
    def __init__(self):
        self.token = None

    def call(self, kernel, outs, *args, scratch=(), smem=0, anywhere=0, flops=0, name=None):
        count, first = len(args), self.token is None
        tokens = [] if first else [self.token]
        results = len(outs)

        def whole(*refs):
            token_out = refs[count + len(tokens) + results]
            token_out[...] = jnp.zeros_like(token_out) if first else refs[count][...]
            outputs = refs[count + len(tokens) : count + len(tokens) + results]
            kernel(*refs[:count], *outputs, *refs[count + len(tokens) + results + 1 :])

        specs = [pl.BlockSpec(memory_space=pltpu.SMEM)] * smem
        specs += [pl.BlockSpec(memory_space=pl.ANY)] * anywhere
        specs += [pl.BlockSpec(memory_space=pltpu.VMEM)] * (count - smem - anywhere + len(tokens))
        size = sum(math.prod(a.shape) * a.dtype.itemsize for a in (*args, *outs))
        *values, self.token = pl.pallas_call(
            whole,
            out_shape=[*outs, shaped((8, LANES), F32)],
            in_specs=specs,
            out_specs=[pl.BlockSpec(memory_space=pltpu.VMEM)] * (results + 1),
            scratch_shapes=list(scratch),
            cost_estimate=pl.CostEstimate(flops=flops, bytes_accessed=size, transcendentals=0),
            compiler_params=pltpu.CompilerParams(vmem_limit_bytes=VMEM_LIMIT),
            name=name,
        )(*args, *tokens)
        return values


def shaped(shape, dtype=BF16):
    return jax.ShapeDtypeStruct(shape, dtype)


def three_pieces(value):
    high = value.astype(BF16)
    rest = value - high.astype(F32)
    middle = rest.astype(BF16)
    low = (rest - middle.astype(F32)).astype(BF16)
    return jnp.concatenate(
        [high.astype(F32), middle.astype(F32), low.astype(F32), jnp.zeros((STAT - 6, LANES), F32)],
        axis=0,
    ).astype(BF16)


def pair_rows(table, pair):
    rows = table[0:2]
    for other in range(1, PAIRS):
        rows = jnp.where(pair == other, table[2 * other : 2 * other + 2], rows)
    return rows


PAY = 544
Q_ROWS = 2 * (GROUP + PAIRS * STAT)
KV_ROWS = 2 * GROUP


def load_kernel(count, source_ref, count_ref, *refs):
    sources, refs = refs[:count], refs[count:]
    loaded, refs = refs[:count], refs[count:]
    send, far, keep, local, total, sem = refs
    copies = [
        pltpu.make_async_copy(source, target, sem.at[i])
        for i, (source, target) in enumerate(zip(sources, loaded))
    ]
    for copy in copies:
        copy.start()
    total[...] = jnp.zeros_like(total)
    copies[0].wait()
    copies[1].wait()
    tiles, grad = loaded[0], loaded[1][...]
    parts = lax.axis_size(NODE)
    home = lax.axis_index(NODE)
    for e in range(tiles.shape[1]):

        @pl.when(e < count_ref[0])
        def _():
            distance = lax.rem(source_ref[0, e] - home + REACH + 2 * parts, parts)
            slot = jnp.clip(distance, 0, 2 * REACH)
            total[slot] += dot(tiles[0, e], grad, TN)

    core = lax.axis_index("c")

    def share(on_first, on_second):
        return total[jnp.where(core == 0, on_first + REACH, on_second + REACH)]

    for i, (on_first, on_second) in enumerate(((-2, 1), (-1, 2), (1, -1))):
        send[i * 128 : (i + 1) * 128] = share(on_first, on_second).astype(BF16)
    for i, (on_first, on_second) in enumerate(((2, -3), (3, -2))):
        keep[i * 128 : (i + 1) * 128] = share(on_first, on_second)
    far[...] = share(-3, 3).astype(BF16)
    local[...] = total[REACH]
    for copy in copies[2:]:
        copy.wait()


def near_kernel(keep, local, received, near, local_out):
    near[...] = (keep[...] + received[0:256].astype(F32)).astype(BF16)
    local_out[...] = local[...] + received[256:384].astype(F32)


def cross_kernel(local, near, far, send, local_out):
    core = lax.axis_index("c")
    mine = pl.ds(pl.multiple_of(core * 128, 128), 128)
    other = pl.ds(pl.multiple_of((1 - core) * 128, 128), 128)
    send[...] = near[other]
    local_out[...] = local[...] + near[mine].astype(F32) + far[...].astype(F32)


def mix_kernel(own_ref, other_ref, weight_ref, mix_ref, q_ref, k_ref, v_ref, log_ref, send, keep, through):
    side = lax.axis_index("h")
    half = own_ref.shape[1]
    own_columns = pl.ds(pl.multiple_of(side * half, half), half)
    other_columns = pl.ds(pl.multiple_of((1 - side) * half, half), half)
    grad = dot(own_ref[...], weight_ref[:, own_columns], NT)
    grad = (grad + dot(other_ref[...], weight_ref[:, other_columns], NT)).astype(BF16)
    product = grad.astype(F32) * mix_ref[...].astype(F32)
    turned_product = product.T
    rows = [jnp.sum(turned_product[64 * i : 64 * (i + 1)], axis=0, keepdims=True) for i in range(8)]
    spread = jnp.concatenate(rows, axis=0)
    logs = log_ref[...]
    me = place_in_group()
    for j, (pay, base) in enumerate(((keep, 0), (send, 0), (through, 0), (send, PAY))):
        pair = me ^ j
        columns = pl.ds(pl.multiple_of(pair * LANES, LANES), LANES)
        block = grad[:, 0:LANES]
        for other in range(1, PAIRS):
            block = jnp.where(pair == other, grad[:, other * LANES : (other + 1) * LANES], block)
        pay[base : base + 128] = q_ref[:, columns]
        pay[base + 128 : base + 144] = three_pieces(pair_rows(logs, pair))
        pay[base + 144 : base + 272] = block
        pay[base + 272 : base + 288] = three_pieces(pair_rows(spread, pair))
        pay[base + 288 : base + 416] = k_ref[:, columns]
        pay[base + 416 : base + 544] = v_ref[:, columns]


def forward_kernel(own, received, out):
    rows = own.shape[0]
    out[0:rows] = own[...]
    out[rows : 2 * rows] = received[rows : 2 * rows]


def join_kernel(own, near, far, q_out, kv_out):
    for j, (pay, base) in enumerate(((own, 0), (near, 0), (far, 0), (far, PAY))):
        for part in range(2):
            at, start = part * (Q_ROWS // 2), base + part * 144
            q_out[at + j * 128 : at + (j + 1) * 128] = pay[start : start + 128]
            stats = at + GROUP + j * STAT
            q_out[stats : stats + STAT] = pay[start + 128 : start + 144]
            start = base + 288 + part * 128
            kv_out[part * GROUP + j * 128 : part * GROUP + (j + 1) * 128] = pay[start : start + 128]


def pair_kernel(first, second, out):
    out[0] = first[...]
    out[1] = second[...]


def masked(block, head):
    lane = lax.broadcasted_iota(jnp.int32, block.shape, 1)
    keep = lane < 64 if head == 0 else lane >= 64
    return jnp.where(keep, block, 0.0).astype(BF16)


def unpack_rows(source, factor, table, stat):
    block = source[0:GROUP].astype(F32) * factor
    for h in range(2):
        table[h] = masked(block, h)
    for j in range(PAIRS):
        pieces = source[GROUP + STAT * j : GROUP + STAT * (j + 1)].astype(F32)
        stat[:, j * LANES : (j + 1) * LANES] = pieces[0:2] + pieces[2:4] + pieces[4:6]


def tile_step(key_tile, value_tile, keys_t, query, grad, logs, spread, dk, dv, dq):
    for h in range(2):
        query_tile, grad_tile = query[h], grad[h]
        scores = dot(key_tile, query_tile, NT) - logs[h : h + 1]
        soft = jnp.exp(scores)
        change = dot(value_tile, grad_tile, NT) - spread[h : h + 1]
        score_grad = (soft * change).astype(BF16)
        dv[...] += dot(soft.astype(BF16), grad_tile, NN)
        dk[...] += dot(score_grad, query_tile, NN)
        head = slice(64 * h, 64 * (h + 1))
        dq[head] += dot(keys_t[head], score_grad, NN)


def turned(block):
    return block.astype(F32).T.astype(BF16)


def attention_kernel(has_dq, has_dkv, dq_last, dkv_last, qdo, kv, *refs):
    if has_dq:
        dq_in, refs = refs[0], refs[1:]
    if has_dkv:
        dkv_in, refs = refs[0], refs[1:]
    dq_out, dkv_out, keys_t, query, grad, logs, spread, dq, dkv = refs
    for i in range(2):
        unpack_rows(qdo.at[i, 0 : Q_ROWS // 2], 0.125, query.at[i], logs.at[i])
        unpack_rows(qdo.at[i, Q_ROWS // 2 : Q_ROWS], 1.0, grad.at[i], spread.at[i])
        keys_t[i] = turned(kv[i, 0:GROUP])
    dq[...] = dq_in[...] if has_dq else jnp.zeros_like(dq)
    dkv[...] = dkv_in[...] if has_dkv else jnp.zeros_like(dkv)

    @pl.loop(0, 4)
    def _(step):
        i, k = step % 2, step // 2
        tile_step(
            kv[k, 0:GROUP],
            kv[k, GROUP : 2 * GROUP],
            keys_t.at[k],
            query.at[i],
            grad.at[i],
            logs.at[i],
            spread.at[i],
            dkv.at[k, pl.ds(0, GROUP)],
            dkv.at[k, pl.ds(GROUP, GROUP)],
            dq.at[i],
        )

    if dq_last:
        for i in range(2):
            dq_out[i] = (dq[i].T * 0.125).astype(dq_out.dtype)
    else:
        dq_out[...] = dq[...]
    dkv_out[...] = dkv[...].astype(dkv_out.dtype)


TILE_FLOPS = 2 * 10 * GROUP * GROUP * 64


def attention(order, name, qdo, kv, dq, dkv, dq_last=None, dkv_last=None):
    carry = [a for a in (dq, dkv) if a is not None]
    dq_shape = (2, LANES, GROUP) if dq_last is None else (2, GROUP, LANES)
    return order.call(
        functools.partial(
            attention_kernel, dq is not None, dkv is not None, dq_last is not None, dkv_last is not None
        ),
        [shaped(dq_shape, dq_last or F32), shaped((2, KV_ROWS, LANES), dkv_last or F32)],
        qdo,
        kv,
        *carry,
        scratch=[
            pltpu.VMEM((2, LANES, GROUP), BF16),
            pltpu.VMEM((2, 2, GROUP, LANES), BF16),
            pltpu.VMEM((2, 2, GROUP, LANES), BF16),
            pltpu.VMEM((2, 2, GROUP), F32),
            pltpu.VMEM((2, 2, GROUP), F32),
            pltpu.VMEM((2, LANES, GROUP), F32),
            pltpu.VMEM((2, KV_ROWS, LANES), F32),
        ],
        flops=4 * TILE_FLOPS,
        name="attention_" + name,
    )


def half_sum_kernel(totals, received, out):
    out[...] = (totals[1].astype(F32) + received[1].astype(F32)).astype(BF16)


def back_kernel(dq, dq_far, dq_near, dkv, dkv_far, dkv_near, send, keep, through):
    dq_sum = (dq[0] + dq_far[0].astype(F32) + dq_near[...].astype(F32)).astype(BF16)
    dkv_sum = (dkv[0] + dkv_far[0].astype(F32) + dkv_near[...].astype(F32)).astype(BF16)
    for j, (pay, base) in enumerate(((keep, 0), (send, 0), (through, 0), (send, 384))):
        pay[base : base + 128] = dq_sum[j * 128 : (j + 1) * 128]
        pay[base + 128 : base + 256] = dkv_sum[j * 128 : (j + 1) * 128]
        pay[base + 256 : base + 384] = dkv_sum[GROUP + j * 128 : GROUP + (j + 1) * 128]


def place_kernel(own, near, far, dq, dk, dv):
    me = place_in_group()
    for j, (pay, base) in enumerate(((own, 0), (near, 0), (far, 0), (far, 384))):
        columns = pl.ds(pl.multiple_of((me ^ j) * LANES, LANES), LANES)
        dq[:, columns] = pay[base : base + 128]
        dk[:, columns] = pay[base + 128 : base + 256]
        dv[:, columns] = pay[base + 256 : base + 384]


def turn_kernel(dq, out):
    for i in range(2):
        out[i] = dq[i].T * 0.125


def weights_kernel(own_ref, other_ref, g_own_ref, g_other_ref, mix_ref, feat_ref, weight_ref, gf_ref, keep_ref, send_ref):
    side = lax.axis_index("h")
    core = lax.axis_index("c")
    half = own_ref.shape[1]
    own_columns = pl.ds(pl.multiple_of(side * half, half), half)
    other_columns = pl.ds(pl.multiple_of((1 - side) * half, half), half)
    features = dot(g_own_ref[...], weight_ref[:, own_columns], NT)
    features = features + dot(g_other_ref[...], weight_ref[:, other_columns], NT)
    gf_ref[...] = features.astype(BF16)
    mix = mix_ref[...].astype(F32).T.astype(BF16)
    feat = feat_ref[...].astype(F32).T.astype(BF16)

    def put(out_refs):
        for left, rights, out in zip((mix, feat), ((own_ref, other_ref), (g_own_ref, g_other_ref)), out_refs):
            out[:, own_columns] = dot(left, rights[0][...], NN).astype(BF16)
            out[:, other_columns] = dot(left, rights[1][...], NN).astype(BF16)

    @pl.when(core == 0)
    def _():
        put((keep_ref, send_ref))

    @pl.when(core == 1)
    def _():
        put((send_ref, keep_ref))


def final_kernel(own_ref, other_ref, first_ref, second_ref):
    core = lax.axis_index("c")

    @pl.when(core == 0)
    def _():
        first_ref[...] = own_ref[...].astype(F32)
        second_ref[...] = other_ref[...].astype(F32)

    @pl.when(core == 1)
    def _():
        first_ref[...] = other_ref[...].astype(F32)
        second_ref[...] = own_ref[...].astype(F32)


def add_kernel(*refs):
    total = refs[0][...].astype(F32)
    for ref in refs[1:-1]:
        total = total + ref[...].astype(F32)
    refs[-1][...] = total.astype(BF16)


def halve_kernel(step, first, second, keep, send):
    rows = keep.shape[0]
    side = side_at("z", step)
    for out, which in ((keep, side), (send, 1 - side)):
        at = pl.ds(pl.multiple_of(which * rows, rows), rows)
        out[...] = (first[at].astype(F32) + second[at].astype(F32)).astype(BF16)


def double_kernel(step, own, received, out):
    rows = own.shape[0]
    side = side_at("z", step)
    out[pl.ds(pl.multiple_of(side * rows, rows), rows)] = own[...]
    out[pl.ds(pl.multiple_of((1 - side) * rows, rows), rows)] = received[...]


def halve(order, step, first, second):
    rows, columns = first.shape
    return order.call(
        functools.partial(halve_kernel, step),
        [shaped((rows // 2, columns))] * 2,
        first,
        second,
        name="halve_%d" % step,
    )


def double(order, step, own, received):
    rows, columns = own.shape
    (out,) = order.call(
        functools.partial(double_kernel, step),
        [shaped((2 * rows, columns))],
        own,
        received,
        name="double_%d" % step,
    )
    return out


def add(order, name, *terms):
    (out,) = order.call(add_kernel, [shaped(terms[0].shape)], *terms, name="add_" + name)
    return out


def pair(order, first, second):
    (out,) = order.call(pair_kernel, [shaped((2,) + first.shape)], first, second, name="pair")
    return out


def body(
    features,
    queries,
    keys,
    values,
    attn_mix,
    log_sums,
    out_weight,
    msg_weight,
    edge_tiles,
    edge_source,
    edge_count,
    out_grad,
):
    rows, columns = out_grad.shape
    order = Order()
    other_grad = swap(out_grad, "h", 1)
    arguments = [edge_tiles, out_grad, queries, keys, values, log_sums, out_weight, attn_mix, features, msg_weight]
    *loaded, share_send, share_far, share_keep, local = order.call(
        functools.partial(load_kernel, len(arguments)),
        [shaped(a.shape, a.dtype) for a in arguments]
        + [
            shaped((3 * rows, columns)),
            shaped((rows, columns)),
            shaped((2 * rows, columns), F32),
            shaped((rows, columns), F32),
        ],
        edge_source,
        edge_count,
        *arguments,
        smem=2,
        anywhere=len(arguments),
        scratch=[
            pltpu.VMEM((2 * REACH + 1, rows, columns), F32),
            pltpu.SemaphoreType.DMA((len(arguments),)),
        ],
        name="load",
    )
    _, out_grad, queries, keys, values, log_sums, out_weight, attn_mix, features, msg_weight = loaded
    share_received = swap(share_send, "c", 1)

    pay_send, pay_own, pay_through = order.call(
        mix_kernel,
        [shaped((2 * PAY, LANES)), shaped((PAY, LANES)), shaped((PAY, LANES))],
        out_grad,
        other_grad,
        out_weight,
        attn_mix,
        queries,
        keys,
        values,
        log_sums,
        name="mix",
    )
    pay_near = swap(pay_send, "c", 1)

    share_near, local = order.call(
        near_kernel,
        [shaped((2 * rows, columns)), shaped((rows, columns), F32)],
        share_keep,
        local,
        share_received,
        name="near",
    )
    parts = lax.axis_size(NODE)
    share_near = lax.ppermute(
        share_near, NODE, [(i, (i + (2 if i % 2 == 0 else -2)) % parts) for i in range(parts)]
    )
    share_far = lax.ppermute(
        share_far, NODE, [(i, (i + (-3 if i % 2 == 0 else 3)) % parts) for i in range(parts)]
    )
    (pay_forward,) = order.call(
        forward_kernel, [shaped((2 * PAY, LANES))], pay_through, pay_near, name="forward"
    )
    pay_far = swap(pay_forward, "y", 1)

    share_cross, local = order.call(
        cross_kernel,
        [shaped((rows, columns)), shaped((rows, columns), F32)],
        local,
        share_near,
        share_far,
        name="cross",
    )
    share_cross = swap(share_cross, "c", 1)

    qdo, kv = order.call(
        join_kernel,
        [shaped((Q_ROWS, LANES)), shaped((KV_ROWS, LANES))],
        pay_own,
        pay_near,
        pay_far,
        name="join",
    )
    qdo_met, kv_met = meet(qdo, "z", 0), meet(kv, "x", 0)

    near_g = add(order, "shares", local, share_cross)
    other_g = swap(near_g, "h", 1)

    qdo_near, kv_near = pair(order, qdo, qdo_met), pair(order, kv, kv_met)
    qdo_far, kv_far = meet(qdo_near, "z", 1), meet(kv_near, "x", 1)

    grad_features, keep, send = order.call(
        weights_kernel,
        [shaped((rows, columns)), shaped((columns, 2 * columns)), shaped((columns, 2 * columns))],
        out_grad,
        other_grad,
        near_g,
        other_g,
        attn_mix,
        features,
        msg_weight,
        name="weights",
    )
    received = swap(send, "c", 1)

    dq_near, dkv_near = attention(order, "near", qdo_near, kv_near, None, None)

    keep, send = halve(order, 0, keep, received)
    received = meet(send, "z", 0)

    dq_far, dkv_far = attention(order, "far", qdo_far, kv_far, None, None)

    keep, send = halve(order, 1, keep, received)
    received = meet(send, "z", 1)

    dq_near, dkv_far = attention(order, "far_keys", qdo_near, kv_far, dq_near, dkv_far, None, BF16)
    dkv_met = meet(dkv_far, "x", 1)

    part = add(order, "z", keep, received)
    received = meet(part, "x", 0)

    dq_far, dkv_near = attention(order, "far_queries", qdo_far, kv_near, dq_far, dkv_near, BF16, F32)
    dq_met = meet(dq_far, "z", 1)
    (dq_near,) = order.call(
        turn_kernel, [shaped((2, GROUP, LANES), F32)], dq_near, name="turn"
    )

    part = add(order, "x0", part, received)
    received = meet(part, "x", 1)
    (half,) = order.call(
        half_sum_kernel, [shaped((KV_ROWS, LANES))], dkv_near, dkv_met, name="half_dkv"
    )
    dkv_last = meet(half, "x", 0)
    part = add(order, "x1", part, received)
    received = swap(part, "y", 1)
    (half,) = order.call(half_sum_kernel, [shaped((GROUP, LANES))], dq_near, dq_met, name="half_dq")
    dq_last = meet(half, "z", 0)
    part = add(order, "y", part, received)
    received = meet(part, "z", 1)

    back_send, back_own, back_through = order.call(
        back_kernel,
        [shaped((768, LANES)), shaped((384, LANES)), shaped((384, LANES))],
        dq_near,
        dq_met,
        dq_last,
        dkv_near,
        dkv_met,
        dkv_last,
        name="back",
    )
    back_near = swap(back_send, "c", 1)
    whole = double(order, 1, part, received)
    received = meet(whole, "z", 0)
    (back_forward,) = order.call(
        forward_kernel, [shaped((768, LANES))], back_through, back_near, name="forward_back"
    )
    back_far = swap(back_forward, "y", 1)
    grad_query, grad_key, grad_value = order.call(
        place_kernel, [shaped((rows, columns))] * 3, back_own, back_near, back_far, name="place"
    )
    whole = double(order, 0, whole, received)
    other = swap(whole, "c", 1)
    out_weight_grad, msg_weight_grad = order.call(
        final_kernel, [shaped(whole.shape, F32)] * 2, whole, other, name="final"
    )
    return (grad_features, grad_query, grad_key, grad_value, out_weight_grad, msg_weight_grad)


def solution(mesh):
    fine = Mesh(mesh.devices.reshape(4, 2, 4, 2, 2), NODE + ("h",))
    both = P(NODE, "h")
    placed = (
        both,
        both,
        both,
        both,
        both,
        P("h", NODE),
        P("h", None),
        P("h", None),
        P(NODE, None, None, None),
        P(NODE, None),
        P(NODE),
        both,
    )
    return jax.shard_map(
        body,
        mesh=fine,
        in_specs=placed,
        out_specs=(both, both, both, both, P("h", None), P("h", None)),
        check_vma=False,
    )
```

```python
import functools
import math

import jax
import jax.numpy as jnp
from jax import lax
from jax.experimental import pallas as pl
from jax.experimental.pallas import tpu as pltpu
from jax.sharding import Mesh
from jax.sharding import PartitionSpec as P

BLOCK = 128
REACH = 3
LANES = 128
PAIRS = 4
STAT = 16
GROUP = 512
NODE = ("z", "y", "x", "c")
BF16 = jnp.bfloat16
F32 = jnp.float32
VMEM_LIMIT = 48 * 1024 * 1024

NT = (((1,), (1,)), ((), ()))
NN = (((1,), (0,)), ((), ()))
TN = (((0,), (0,)), ((), ()))


def dot(a, b, dims):
    return lax.dot_general(a, b, dims, preferred_element_type=F32)


def swap(value, axes, mask):
    count = lax.axis_size(axes)
    return lax.ppermute(value, axes, [(i, i ^ mask) for i in range(count)])


NEXT = ((1, 0, 3, 2), (3, 2, 1, 0))


def meet(value, axis, step):
    pairs = [
        (2 * i + core, 2 * NEXT[(step + core) % 2][i] + core) for i in range(4) for core in range(2)
    ]
    return lax.ppermute(value, (axis, "c"), pairs)


def x_near(value):
    pairs = [(2 * i + c, 2 * ((i + (1 if c == 0 else 3)) % 4) + c) for i in range(4) for c in range(2)]
    return lax.ppermute(value, ("x", "c"), pairs)


def x_far(value):
    return swap(value, "x", 2)


def place_in_group():
    return lax.axis_index("y") * 2 + lax.axis_index("c")


class Order:
    def __init__(self):
        self.token = None

    def call(self, kernel, outs, *args, scratch=(), smem=0, anywhere=0, flops=0, name=None):
        count, first = len(args), self.token is None
        tokens = [] if first else [self.token]
        results = len(outs)

        def whole(*refs):
            token_out = refs[count + len(tokens) + results]
            token_out[...] = jnp.zeros_like(token_out) if first else refs[count][...]
            outputs = refs[count + len(tokens) : count + len(tokens) + results]
            kernel(*refs[:count], *outputs, *refs[count + len(tokens) + results + 1 :])

        specs = [pl.BlockSpec(memory_space=pltpu.SMEM)] * smem
        specs += [pl.BlockSpec(memory_space=pltpu.HBM)] * anywhere
        specs += [pl.BlockSpec(memory_space=pltpu.VMEM)] * (count - smem - anywhere + len(tokens))
        size = sum(math.prod(a.shape) * a.dtype.itemsize for a in (*args, *outs))
        *values, self.token = pl.pallas_call(
            whole,
            out_shape=[*outs, shaped((8, LANES), F32)],
            in_specs=specs,
            out_specs=[pl.BlockSpec(memory_space=pltpu.VMEM)] * (results + 1),
            scratch_shapes=list(scratch),
            cost_estimate=pl.CostEstimate(flops=flops, bytes_accessed=size, transcendentals=0),
            compiler_params=pltpu.CompilerParams(vmem_limit_bytes=VMEM_LIMIT),
            name=name,
        )(*args, *tokens)
        return values


def shaped(shape, dtype=BF16):
    return jax.ShapeDtypeStruct(shape, dtype)


def three_pieces(value):
    high = value.astype(BF16)
    rest = value - high.astype(F32)
    middle = rest.astype(BF16)
    low = (rest - middle.astype(F32)).astype(BF16)
    return jnp.concatenate(
        [high.astype(F32), middle.astype(F32), low.astype(F32), jnp.zeros((STAT - 6, LANES), F32)],
        axis=0,
    ).astype(BF16)


def pair_rows(table, pair):
    rows = table[0:2]
    for other in range(1, PAIRS):
        rows = jnp.where(pair == other, table[2 * other : 2 * other + 2], rows)
    return rows


Q_PAY = 288
KV_PAY = 256
Q_ROWS = 2 * (GROUP + PAIRS * STAT)
KV_ROWS = 2 * GROUP


def load_kernel(count, *refs):
    sem = refs[-1]
    copies = [
        pltpu.make_async_copy(source, target, sem.at[i])
        for i, (source, target) in enumerate(zip(refs[:count], refs[count : 2 * count]))
    ]
    for copy in copies:
        copy.start()
    for copy in copies:
        copy.wait()


def whole_rows(own, other, out):
    side, half = lax.axis_index("h"), own.shape[1]
    out[:, pl.ds(pl.multiple_of(side * half, half), half)] = own[...]
    out[:, pl.ds(pl.multiple_of((1 - side) * half, half), half)] = other[...]


def slot_of(source_ref, e):
    parts = lax.axis_size(NODE)
    distance = lax.rem(source_ref[0, e] - lax.axis_index(NODE) + REACH + 2 * parts, parts)
    return jnp.clip(distance, 0, 2 * REACH)


def chip_kernel(own, other, out):
    core = lax.axis_index("c")
    out[pl.ds(pl.multiple_of(core * 128, 128), 128)] = own[...]
    out[pl.ds(pl.multiple_of((1 - core) * 128, 128), 128)] = other[...]


def share_kernel(source_ref, count_ref, tiles, grad, weight, send, far, keep, local, total):
    total[...] = jnp.zeros_like(total)
    grad_aggregate = dot(grad[...], weight[...], NT).astype(BF16)
    for e in range(tiles.shape[1]):

        @pl.when(e < count_ref[0])
        def _():
            total[slot_of(source_ref, e)] += dot(tiles[0, e], grad_aggregate, TN)

    core = lax.axis_index("c")

    def share(on_first, on_second):
        return total[jnp.where(core == 0, on_first + REACH, on_second + REACH)]

    for i, (on_first, on_second) in enumerate(((-2, 1), (-1, 2), (1, -1))):
        send[i * 128 : (i + 1) * 128] = share(on_first, on_second).astype(BF16)
    for i, (on_first, on_second) in enumerate(((2, -3), (3, -2))):
        keep[i * 128 : (i + 1) * 128] = share(on_first, on_second)
    far[...] = share(-3, 3).astype(BF16)
    local[...] = total[REACH]


def near_kernel(keep, local, received, near, local_out):
    near[...] = (keep[...] + received[0:256].astype(F32)).astype(BF16)
    local_out[...] = local[...] + received[256:384].astype(F32)


def cross_kernel(local, near, far, send, local_out):
    core = lax.axis_index("c")
    mine = pl.ds(pl.multiple_of(core * 128, 128), 128)
    other = pl.ds(pl.multiple_of((1 - core) * 128, 128), 128)
    send[...] = near[other]
    local_out[...] = local[...] + near[mine].astype(F32) + far[...].astype(F32)


def pay_kernel(k_ref, v_ref, *pays):
    me = place_in_group()
    for j, pay in enumerate(pays):
        columns = pl.ds(pl.multiple_of((me ^ j) * LANES, LANES), LANES)
        pay[0:128] = k_ref[:, columns]
        pay[128:256] = v_ref[:, columns]


def mix_kernel(own, other, weight_ref, mix_ref, q_ref, log_ref, whole, *pays):
    whole_rows(own, other, whole)
    grad = dot(whole[...], weight_ref[...], NT).astype(BF16)
    product = grad.astype(F32) * mix_ref[...].astype(F32)
    turned_product = product.T
    rows = [jnp.sum(turned_product[64 * i : 64 * (i + 1)], axis=0, keepdims=True) for i in range(8)]
    spread = jnp.concatenate(rows, axis=0)
    logs = log_ref[...]
    me = place_in_group()
    for j, pay in enumerate(pays):
        pair = me ^ j
        columns = pl.ds(pl.multiple_of(pair * LANES, LANES), LANES)
        block = grad[:, 0:LANES]
        for other in range(1, PAIRS):
            block = jnp.where(pair == other, grad[:, other * LANES : (other + 1) * LANES], block)
        pay[0:128] = q_ref[:, columns]
        pay[128:144] = three_pieces(pair_rows(logs, pair))
        pay[144:272] = block
        pay[272:288] = three_pieces(pair_rows(spread, pair))


def forward_kernel(own, received, out):
    rows = own.shape[0]
    out[0:rows] = own[...]
    out[rows : 2 * rows] = received[...]


def join_rows_kernel(own, near, far, out):
    for j, (pay, base) in enumerate(((own, 0), (near, 0), (far, 0), (far, Q_PAY))):
        for part in range(2):
            at, start = part * (Q_ROWS // 2), base + part * 144
            out[at + j * 128 : at + (j + 1) * 128] = pay[start : start + 128]
            stats = at + GROUP + j * STAT
            out[stats : stats + STAT] = pay[start + 128 : start + 144]


def join_keys_kernel(own, near, far, out):
    for j, (pay, base) in enumerate(((own, 0), (near, 0), (far, 0), (far, KV_PAY))):
        for part in range(2):
            start = base + part * 128
            out[part * GROUP + j * 128 : part * GROUP + (j + 1) * 128] = pay[start : start + 128]


def pair_kernel(first, second, out):
    out[0] = first[...]
    out[1] = second[...]


def masked(block, head):
    lane = lax.broadcasted_iota(jnp.int32, block.shape, 1)
    keep = lane < 64 if head == 0 else lane >= 64
    return jnp.where(keep, block, 0.0).astype(BF16)


def unpack_rows(source, factor, table, stat):
    block = source[0:GROUP].astype(F32) * factor
    for h in range(2):
        table[h] = masked(block, h)
    for j in range(PAIRS):
        pieces = source[GROUP + STAT * j : GROUP + STAT * (j + 1)].astype(F32)
        stat[:, j * LANES : (j + 1) * LANES] = pieces[0:2] + pieces[2:4] + pieces[4:6]


def tile_step(key_tile, value_tile, keys_t, query, grad, logs, spread, dk, dv, dq):
    for h in range(2):
        query_tile, grad_tile = query[h], grad[h]
        scores = dot(key_tile, query_tile, NT) - logs[h : h + 1]
        soft = jnp.exp(scores)
        change = dot(value_tile, grad_tile, NT) - spread[h : h + 1]
        score_grad = (soft * change).astype(BF16)
        dv[...] += dot(soft.astype(BF16), grad_tile, NN)
        dk[...] += dot(score_grad, query_tile, NN)
        head = slice(64 * h, 64 * (h + 1))
        dq[head] += dot(keys_t[head], score_grad, NN)


def turned(block):
    return block.astype(F32).T.astype(BF16)


def attention_kernel(has_dq, has_dkv, dq_last, dkv_last, qdo, kv, *refs):
    if has_dq:
        dq_in, refs = refs[0], refs[1:]
    if has_dkv:
        dkv_in, refs = refs[0], refs[1:]
    dq_out, dkv_out, keys_t, query, grad, logs, spread, dq, dkv = refs
    for i in range(2):
        unpack_rows(qdo.at[i, 0 : Q_ROWS // 2], 0.125, query.at[i], logs.at[i])
        unpack_rows(qdo.at[i, Q_ROWS // 2 : Q_ROWS], 1.0, grad.at[i], spread.at[i])
        keys_t[i] = turned(kv[i, 0:GROUP])
    dq[...] = dq_in[...] if has_dq else jnp.zeros_like(dq)
    dkv[...] = dkv_in[...] if has_dkv else jnp.zeros_like(dkv)

    @pl.loop(0, 4)
    def _(step):
        i, k = step % 2, step // 2
        tile_step(
            kv[k, 0:GROUP],
            kv[k, GROUP : 2 * GROUP],
            keys_t.at[k],
            query.at[i],
            grad.at[i],
            logs.at[i],
            spread.at[i],
            dkv.at[k, pl.ds(0, GROUP)],
            dkv.at[k, pl.ds(GROUP, GROUP)],
            dq.at[i],
        )

    if dq_last:
        for i in range(2):
            dq_out[i] = (dq[i].T * 0.125).astype(dq_out.dtype)
    else:
        dq_out[...] = dq[...]
    dkv_out[...] = dkv[...].astype(dkv_out.dtype)


SLOW = 10**10
MIX = SLOW
JOIN = SLOW
JOIN_KEYS = 1 * 10**9
FORWARD = 0
PAIR = SLOW
WEIGHTS = 0
TILE_FLOPS = 2 * 10 * GROUP * GROUP * 64


def attention(order, name, qdo, kv, dq, dkv, dq_last=None, dkv_last=None):
    carry = [a for a in (dq, dkv) if a is not None]
    dq_shape = (2, LANES, GROUP) if dq_last is None else (2, GROUP, LANES)
    return order.call(
        functools.partial(
            attention_kernel, dq is not None, dkv is not None, dq_last is not None, dkv_last is not None
        ),
        [shaped(dq_shape, dq_last or F32), shaped((2, KV_ROWS, LANES), dkv_last or F32)],
        qdo,
        kv,
        *carry,
        scratch=[
            pltpu.VMEM((2, LANES, GROUP), BF16),
            pltpu.VMEM((2, 2, GROUP, LANES), BF16),
            pltpu.VMEM((2, 2, GROUP, LANES), BF16),
            pltpu.VMEM((2, 2, GROUP), F32),
            pltpu.VMEM((2, 2, GROUP), F32),
            pltpu.VMEM((2, LANES, GROUP), F32),
            pltpu.VMEM((2, KV_ROWS, LANES), F32),
        ],
        flops=4 * TILE_FLOPS,
        name="attention_" + name,
    )


def half_sum_kernel(totals, received, out):
    out[...] = (totals[1].astype(F32) + received[1].astype(F32)).astype(BF16)


def back_kernel(dq, dq_far, dq_near, dkv, dkv_far, dkv_near, keep, near, through, far):
    dq_sum = (dq[0] + dq_far[0].astype(F32) + dq_near[...].astype(F32)).astype(BF16)
    dkv_sum = (dkv[0] + dkv_far[0].astype(F32) + dkv_near[...].astype(F32)).astype(BF16)
    for j, (pay, base) in enumerate(((keep, 0), (near, 0), (through, 0), (far, 0))):
        pay[base : base + 128] = dq_sum[j * 128 : (j + 1) * 128]
        pay[base + 128 : base + 256] = dkv_sum[j * 128 : (j + 1) * 128]
        pay[base + 256 : base + 384] = dkv_sum[GROUP + j * 128 : GROUP + (j + 1) * 128]


def place_kernel(own, near, far, dq, dk, dv):
    me = place_in_group()
    for j, (pay, base) in enumerate(((own, 0), (near, 0), (far, 0), (far, 384))):
        columns = pl.ds(pl.multiple_of((me ^ j) * LANES, LANES), LANES)
        dq[:, columns] = pay[base : base + 128]
        dk[:, columns] = pay[base + 128 : base + 256]
        dv[:, columns] = pay[base + 256 : base + 384]


def turn_kernel(dq, out):
    for i in range(2):
        out[i] = dq[i].T * 0.125


def weights_kernel(source_ref, count_ref, tiles, grad, mix_ref, own, partner, near, crossed, far, keep_ref, send_ref, window, total, left_ref):
    core = lax.axis_index("c")
    place = lax.axis_index("x")
    window[REACH] = own[...]
    window[jnp.where(core == 0, 4, 2)] = partner[...]
    for block, first in ((near, jnp.where(core == 0, 1, 4)), (crossed, jnp.where(core == 0, 5, 0))):
        window[first] = block[0:128]
        window[first + 1] = block[128:256]
    window[6 * core] = far[...]
    total[...] = jnp.zeros_like(total)
    for e in range(tiles.shape[1]):

        @pl.when(e < count_ref[0])
        def _():
            total[...] += dot(tiles[0, e], window[slot_of(source_ref, e)], NN)

    left_ref[0] = turned(mix_ref[...])
    left_ref[1] = turned(total[...].astype(BF16))

    def put(out, slot, which, distance):
        rows = pl.ds(pl.multiple_of(lax.rem(place + distance, 4) * 128, 128), 128)
        out[slot * 128 : (slot + 1) * 128] = dot(left_ref[which, rows], grad[...], NN).astype(BF16)

    for out, turn in ((keep_ref, core), (send_ref, 1 - core)):
        ahead = jnp.where(turn == 0, 1, 3)
        put(out, 0, 0, ahead)
        put(out, 1, 1, ahead)
        put(out, 2, turn, 2)
        put(out, 3, turn, 0)


def core_sum_kernel(keep, received, near, far, local):
    near[...] = (keep[0:256].astype(F32) + received[0:256].astype(F32)).astype(BF16)
    far[...] = (keep[256:384].astype(F32) + received[256:384].astype(F32)).astype(BF16)
    local[...] = keep[384:512].astype(F32) + received[384:512].astype(F32)


def core_split_kernel(local, near, far, send, local_out):
    core = lax.axis_index("c")
    mine = pl.ds(pl.multiple_of(core * 128, 128), 128)
    other = pl.ds(pl.multiple_of((1 - core) * 128, 128), 128)
    send[...] = near[other]
    local_out[...] = local[...] + near[mine].astype(F32) + far[...].astype(F32)


def core_pack_kernel(own, received, out):
    core = lax.axis_index("c")
    out[pl.ds(pl.multiple_of(core * 128, 128), 128)] = own[...]
    out[pl.ds(pl.multiple_of((1 - core) * 128, 128), 128)] = received[...]


def core_send_kernel(near, far, out):
    out[0:256] = near[...]
    out[256:384] = far[...]


def final_kernel(local, near, received, first_ref, second_ref):
    core = lax.axis_index("c")
    place = lax.axis_index("x")

    def rows(distance):
        return pl.ds(pl.multiple_of(lax.rem(place + distance, 4) * 128, 128), 128)

    before = jnp.where(core == 0, 3, 1)
    outs = (first_ref, second_ref)
    for i, out in enumerate(outs):
        block = slice(i * 128, (i + 1) * 128)
        out[rows(0)] = local[block].astype(F32)
        out[rows(before)] = near[block].astype(F32)
        out[rows(4 - before)] = received[block].astype(F32)

    @pl.when(core == 0)
    def _():
        first_ref[rows(2)] = near[256:384].astype(F32)
        second_ref[rows(2)] = received[256:384].astype(F32)

    @pl.when(core == 1)
    def _():
        second_ref[rows(2)] = near[256:384].astype(F32)
        first_ref[rows(2)] = received[256:384].astype(F32)


def add_kernel(*refs):
    total = refs[0][...].astype(F32)
    for ref in refs[1:-1]:
        total = total + ref[...].astype(F32)
    refs[-1][...] = total.astype(BF16)


def add(order, name, *terms):
    (out,) = order.call(add_kernel, [shaped(terms[0].shape)], *terms, name="add_" + name)
    return out


def pair(order, first, second):
    (out,) = order.call(pair_kernel, [shaped((2,) + first.shape)], first, second, flops=PAIR, name="pair")
    return out


def body(
    features,
    queries,
    keys,
    values,
    attn_mix,
    log_sums,
    out_weight,
    msg_weight,
    edge_tiles,
    edge_source,
    edge_count,
    out_grad,
):
    rows, columns = out_grad.shape
    order = Order()
    other_grad = swap(out_grad, "h", 1)
    parts = lax.axis_size(NODE)
    to_near = [(i, (i + (2 if i % 2 == 0 else -2)) % parts) for i in range(parts)]
    to_far = [(i, (i + (-3 if i % 2 == 0 else 3)) % parts) for i in range(parts)]
    partner_features = swap(features, "c", 1)
    far_features = lax.ppermute(features, NODE, to_far)
    arguments = [features, edge_tiles, out_grad, queries, keys, values, log_sums, out_weight, attn_mix, msg_weight]
    arguments = [pltpu.with_memory_space_constraint(a, pltpu.HBM) for a in arguments]
    loaded = order.call(
        functools.partial(load_kernel, len(arguments)),
        [shaped(a.shape, a.dtype) for a in arguments],
        *arguments,
        anywhere=len(arguments),
        scratch=[pltpu.SemaphoreType.DMA((len(arguments),))],
        name="load",
    )
    features, edge_tiles, out_grad, queries, keys, values, log_sums, out_weight, attn_mix, msg_weight = loaded
    wide = (rows, 2 * columns)
    key_pays = order.call(
        pay_kernel, [shaped((KV_PAY, LANES))] * 4, keys, values, name="pay"
    )
    key_near, key_cross = swap(key_pays[1], "c", 1), swap(key_pays[3], "c", 1)
    (near_features,) = order.call(
        chip_kernel, [shaped((2 * rows, columns))], features, partner_features, name="chip"
    )
    near_features = lax.ppermute(near_features, NODE, to_near)
    (key_far,) = order.call(
        forward_kernel, [shaped((2 * KV_PAY, LANES))], key_pays[2], key_cross, name="forward_keys"
    )
    key_far = swap(key_far, "y", 1)
    out_grad, *pays = order.call(
        mix_kernel,
        [shaped(wide)] + [shaped((Q_PAY, LANES))] * 4,
        out_grad,
        other_grad,
        out_weight,
        attn_mix,
        queries,
        log_sums,
        flops=MIX,
        name="mix",
    )
    pay_near, pay_cross = swap(pays[1], "c", 1), swap(pays[3], "c", 1)
    (pay_far,) = order.call(
        forward_kernel, [shaped((2 * Q_PAY, LANES))], pays[2], pay_cross, flops=FORWARD, name="forward"
    )
    pay_far = swap(pay_far, "y", 1)
    (kv,) = order.call(
        join_keys_kernel,
        [shaped((KV_ROWS, LANES))],
        key_pays[0],
        key_near,
        key_far,
        flops=JOIN_KEYS,
        name="join_keys",
    )
    kv_met = meet(kv, "x", 0)
    (qdo,) = order.call(
        join_rows_kernel,
        [shaped((Q_ROWS, LANES))],
        pays[0],
        pay_near,
        pay_far,
        flops=JOIN,
        name="join",
    )
    qdo_met = meet(qdo, "z", 0)
    crossed_features = swap(near_features, "c", 1)
    keep, send = order.call(
        weights_kernel,
        [shaped((columns, 2 * columns)), shaped((columns, 2 * columns))],
        edge_source,
        edge_count,
        edge_tiles,
        out_grad,
        attn_mix,
        features,
        partner_features,
        near_features,
        crossed_features,
        far_features,
        smem=2,
        scratch=[
            pltpu.VMEM((2 * REACH + 1, rows, columns), BF16),
            pltpu.VMEM((rows, columns), F32),
            pltpu.VMEM((2, columns, rows), BF16),
        ],
        flops=WEIGHTS,
        name="weights",
    )
    received = swap(send, "c", 1)
    kv_near = pair(order, kv, kv_met)
    kv_far = meet(kv_near, "x", 1)
    qdo_near = pair(order, qdo, qdo_met)
    qdo_far = meet(qdo_near, "z", 1)
    near, far, local = order.call(
        core_sum_kernel,
        [shaped((2 * rows, 2 * columns)), shaped(wide), shaped(wide, F32)],
        keep,
        received,
        name="core_sum",
    )
    far, near = x_far(far), x_near(near)

    share_send, share_far, share_keep, share_local = order.call(
        share_kernel,
        [
            shaped((3 * rows, columns)),
            shaped((rows, columns)),
            shaped((2 * rows, columns), F32),
            shaped((rows, columns), F32),
        ],
        edge_source,
        edge_count,
        edge_tiles,
        out_grad,
        msg_weight,
        smem=2,
        scratch=[pltpu.VMEM((2 * REACH + 1, rows, columns), F32)],
        name="shares",
    )
    share_received = swap(share_send, "c", 1)
    dq_near, dkv_near = attention(order, "near", qdo_near, kv_near, None, None)
    dq_far, dkv_far = attention(order, "far", qdo_far, kv_far, None, None)
    send, local = order.call(
        core_split_kernel, [shaped(wide), shaped(wide, F32)], local, near, far, name="core_split"
    )
    received = swap(send, "c", 1)
    part = add(order, "x", local, received)
    received = meet(part, "z", 0)
    share_near, share_local = order.call(
        near_kernel,
        [shaped((2 * rows, columns)), shaped((rows, columns), F32)],
        share_keep,
        share_local,
        share_received,
        name="near",
    )
    share_far, share_near = lax.ppermute(share_far, NODE, to_far), lax.ppermute(share_near, NODE, to_near)
    dq_near, dkv_far = attention(order, "far_keys", qdo_near, kv_far, dq_near, dkv_far, None, BF16)
    dkv_met = meet(dkv_far, "x", 1)
    part = add(order, "z0", part, received)
    received = meet(part, "z", 1)
    share_cross, share_local = order.call(
        cross_kernel,
        [shaped((rows, columns)), shaped((rows, columns), F32)],
        share_local,
        share_near,
        share_far,
        flops=SLOW,
        name="cross",
    )
    share_cross = swap(share_cross, "c", 1)
    dq_far, dkv_near = attention(order, "far_queries", qdo_far, kv_near, dq_far, dkv_near, BF16, F32)
    dq_met = meet(dq_far, "z", 1)
    part = add(order, "z1", part, received)
    received = swap(part, "y", 1)
    grad_features = add(order, "shares", share_local, share_cross)
    (half,) = order.call(
        half_sum_kernel, [shaped((KV_ROWS, LANES))], dkv_near, dkv_met, name="half_dkv"
    )
    dkv_last = meet(half, "x", 0)
    (dq_near,) = order.call(
        turn_kernel, [shaped((2, GROUP, LANES), F32)], dq_near, name="turn"
    )
    part = add(order, "y", part, received)
    far, received = x_far(part), swap(part, "c", 1)
    (half,) = order.call(half_sum_kernel, [shaped((GROUP, LANES))], dq_near, dq_met, name="half_dq")
    dq_last = meet(half, "z", 0)
    (local,) = order.call(
        core_pack_kernel, [shaped((2 * rows, 2 * columns))], part, received, name="core_pack"
    )
    near = x_near(local)

    back_own, back_near, back_through, back_cross = order.call(
        back_kernel,
        [shaped((384, LANES))] * 4,
        dq_near,
        dq_met,
        dq_last,
        dkv_near,
        dkv_met,
        dkv_last,
        name="back",
    )
    back_near, back_cross = swap(back_near, "c", 1), swap(back_cross, "c", 1)
    (back_forward,) = order.call(
        forward_kernel, [shaped((768, LANES))], back_through, back_cross, name="forward_back"
    )
    back_far = swap(back_forward, "y", 1)
    grad_query, grad_key, grad_value = order.call(
        place_kernel, [shaped((rows, columns))] * 3, back_own, back_near, back_far, name="place"
    )
    (near,) = order.call(
        core_send_kernel, [shaped((3 * rows, 2 * columns))], near, far, name="core_send"
    )
    out_weight_grad, msg_weight_grad = order.call(
        final_kernel,
        [shaped((columns, 2 * columns), F32)] * 2,
        local,
        near,
        swap(near, "c", 1),
        name="final",
    )
    return (grad_features, grad_query, grad_key, grad_value, out_weight_grad, msg_weight_grad)


def solution(mesh):
    fine = Mesh(mesh.devices.reshape(4, 2, 4, 2, 2), NODE + ("h",))
    both = P(NODE, "h")
    placed = (
        both,
        both,
        both,
        both,
        both,
        P("h", NODE),
        P("h", None),
        P("h", None),
        P(NODE, None, None, None),
        P(NODE, None),
        P(NODE),
        both,
    )
    return jax.shard_map(
        body,
        mesh=fine,
        in_specs=placed,
        out_specs=(both, both, both, both, P("h", None), P("h", None)),
        check_vma=False,
    )
```

```python
import functools
import math

import jax
import jax.numpy as jnp
from jax import lax
from jax.experimental import pallas as pl
from jax.experimental.pallas import tpu as pltpu
from jax.sharding import Mesh
from jax.sharding import PartitionSpec as P

BLOCK = 128
REACH = 3
LANES = 128
PAIRS = 4
STAT = 16
GROUP = 512
NODE = ("z", "y", "x", "c")
BF16 = jnp.bfloat16
F32 = jnp.float32
VMEM_LIMIT = 48 * 1024 * 1024

NT = (((1,), (1,)), ((), ()))
NN = (((1,), (0,)), ((), ()))
TN = (((0,), (0,)), ((), ()))


def dot(a, b, dims):
    return lax.dot_general(a, b, dims, preferred_element_type=F32)


def swap(value, axes, mask):
    count = lax.axis_size(axes)
    return lax.ppermute(value, axes, [(i, i ^ mask) for i in range(count)])


NEXT = ((1, 0, 3, 2), (3, 2, 1, 0))


def meet(value, axis, step):
    pairs = [
        (2 * i + core, 2 * NEXT[(step + core) % 2][i] + core) for i in range(4) for core in range(2)
    ]
    return lax.ppermute(value, (axis, "c"), pairs)


def ring_place():
    return jnp.where(lax.axis_index("c") == 0, lax.axis_index("x"), lax.axis_index("z"))


def ring(value, to_first, to_second):
    pairs = []
    for z in range(4):
        for x in range(4):
            pairs.append((8 * z + 2 * x, 8 * to_first[1][z] + 2 * to_first[0][x]))
            pairs.append((8 * z + 2 * x + 1, 8 * to_second[1][z] + 2 * to_second[0][x] + 1))
    return lax.ppermute(value, ("z", "x", "c"), pairs)


STAY = (0, 1, 2, 3)


def around(value, steps):
    turn = tuple((i + steps) % 4 for i in range(4))
    return ring(value, (turn, STAY), (STAY, turn))


def across(value, step):
    return ring(value, (STAY, NEXT[step]), (NEXT[step], STAY))


def place_in_group():
    return lax.axis_index("y") * 2 + lax.axis_index("c")


class Order:
    def __init__(self):
        self.token = None

    def call(self, kernel, outs, *args, scratch=(), smem=0, anywhere=0, aliases={}, flops=0, name=None):
        count, first = len(args), self.token is None
        tokens = [] if first else [self.token]
        results = len(outs)

        def whole(*refs):
            token_out = refs[count + len(tokens) + results]
            token_out[...] = jnp.zeros_like(token_out) if first else refs[count][...]
            outputs = refs[count + len(tokens) : count + len(tokens) + results]
            kernel(*refs[:count], *outputs, *refs[count + len(tokens) + results + 1 :])

        specs = [pl.BlockSpec(memory_space=pltpu.SMEM)] * smem
        specs += [pl.BlockSpec(memory_space=pltpu.HBM)] * anywhere
        specs += [pl.BlockSpec(memory_space=pltpu.VMEM)] * (count - smem - anywhere + len(tokens))
        size = sum(math.prod(a.shape) * a.dtype.itemsize for a in (*args, *outs))
        *values, self.token = pl.pallas_call(
            whole,
            out_shape=[*outs, shaped((8, LANES), F32)],
            in_specs=specs,
            out_specs=[pl.BlockSpec(memory_space=pltpu.VMEM)] * (results + 1),
            scratch_shapes=list(scratch),
            input_output_aliases=aliases,
            cost_estimate=pl.CostEstimate(flops=flops, bytes_accessed=size, transcendentals=0),
            compiler_params=pltpu.CompilerParams(vmem_limit_bytes=VMEM_LIMIT),
            name=name,
        )(*args, *tokens)
        return values


def shaped(shape, dtype=BF16):
    return jax.ShapeDtypeStruct(shape, dtype)


def three_pieces(value):
    high = value.astype(BF16)
    rest = value - high.astype(F32)
    middle = rest.astype(BF16)
    low = (rest - middle.astype(F32)).astype(BF16)
    return jnp.concatenate(
        [high.astype(F32), middle.astype(F32), low.astype(F32), jnp.zeros((STAT - 6, LANES), F32)],
        axis=0,
    ).astype(BF16)


def pair_rows(table, pair):
    rows = table[0:2]
    for other in range(1, PAIRS):
        rows = jnp.where(pair == other, table[2 * other : 2 * other + 2], rows)
    return rows


Q_PAY = 288
KV_PAY = 256
Q_ROWS = 2 * (GROUP + PAIRS * STAT)
KV_ROWS = 2 * GROUP


def load_kernel(count, *refs):
    sem = refs[-1]
    copies = [
        pltpu.make_async_copy(source, target, sem.at[i])
        for i, (source, target) in enumerate(zip(refs[:count], refs[count : 2 * count]))
    ]
    for copy in copies:
        copy.start()
    for copy in copies:
        copy.wait()


def whole_rows(own, other, out):
    side, half = lax.axis_index("h"), own.shape[1]
    out[:, pl.ds(pl.multiple_of(side * half, half), half)] = own[...]
    out[:, pl.ds(pl.multiple_of((1 - side) * half, half), half)] = other[...]


def slot_of(source_ref, e):
    parts = lax.axis_size(NODE)
    distance = lax.rem(source_ref[0, e] - lax.axis_index(NODE) + REACH + 2 * parts, parts)
    return jnp.clip(distance, 0, 2 * REACH)


def chip_kernel(own, other, out):
    core = lax.axis_index("c")
    out[pl.ds(pl.multiple_of(core * 128, 128), 128)] = own[...]
    out[pl.ds(pl.multiple_of((1 - core) * 128, 128), 128)] = other[...]


def share_kernel(source_ref, count_ref, tiles, grad, weight, send, far, keep, local, total):
    total[...] = jnp.zeros_like(total)
    grad_aggregate = dot(grad[...], weight[...], NT).astype(BF16)
    for e in range(tiles.shape[1]):

        @pl.when(e < count_ref[0])
        def _():
            total[slot_of(source_ref, e)] += dot(tiles[0, e], grad_aggregate, TN)

    core = lax.axis_index("c")

    def share(on_first, on_second):
        return total[jnp.where(core == 0, on_first + REACH, on_second + REACH)]

    for i, (on_first, on_second) in enumerate(((-2, 1), (-1, 2), (1, -1))):
        send[i * 128 : (i + 1) * 128] = share(on_first, on_second).astype(BF16)
    for i, (on_first, on_second) in enumerate(((2, -3), (3, -2))):
        keep[i * 128 : (i + 1) * 128] = share(on_first, on_second)
    far[...] = share(-3, 3).astype(BF16)
    local[...] = total[REACH]


def near_kernel(keep, local, received, near, local_out):
    near[...] = (keep[...] + received[0:256].astype(F32)).astype(BF16)
    local_out[...] = local[...] + received[256:384].astype(F32)


def cross_kernel(local, near, far, send, local_out):
    core = lax.axis_index("c")
    mine = pl.ds(pl.multiple_of(core * 128, 128), 128)
    other = pl.ds(pl.multiple_of((1 - core) * 128, 128), 128)
    send[...] = near[other]
    local_out[...] = local[...] + near[mine].astype(F32) + far[...].astype(F32)


def pay_kernel(k_ref, v_ref, *pays):
    me = place_in_group()
    for j, pay in enumerate(pays):
        columns = pl.ds(pl.multiple_of((me ^ j) * LANES, LANES), LANES)
        pay[0:128] = k_ref[:, columns]
        pay[128:256] = v_ref[:, columns]


def mix_kernel(own, other, weight_ref, mix_ref, q_ref, log_ref, whole, *pays):
    whole_rows(own, other, whole)
    grad = dot(whole[...], weight_ref[...], NT).astype(BF16)
    product = grad.astype(F32) * mix_ref[...].astype(F32)
    turned_product = product.T
    rows = [jnp.sum(turned_product[64 * i : 64 * (i + 1)], axis=0, keepdims=True) for i in range(8)]
    spread = jnp.concatenate(rows, axis=0)
    logs = log_ref[...]
    me = place_in_group()
    for j, pay in enumerate(pays):
        pair = me ^ j
        columns = pl.ds(pl.multiple_of(pair * LANES, LANES), LANES)
        block = grad[:, 0:LANES]
        for other in range(1, PAIRS):
            block = jnp.where(pair == other, grad[:, other * LANES : (other + 1) * LANES], block)
        pay[0:128] = q_ref[:, columns]
        pay[128:144] = three_pieces(pair_rows(logs, pair))
        pay[144:272] = block
        pay[272:288] = three_pieces(pair_rows(spread, pair))


def forward_kernel(own, received, out):
    rows = own.shape[0]
    out[0:rows] = own[...]
    out[rows : 2 * rows] = received[...]


def join_rows_kernel(own, near, far, out):
    for j, (pay, base) in enumerate(((own, 0), (near, 0), (far, 0), (far, Q_PAY))):
        for part in range(2):
            at, start = part * (Q_ROWS // 2), base + part * 144
            out[at + j * 128 : at + (j + 1) * 128] = pay[start : start + 128]
            stats = at + GROUP + j * STAT
            out[stats : stats + STAT] = pay[start + 128 : start + 144]


def join_keys_kernel(own, near, far, out):
    for j, (pay, base) in enumerate(((own, 0), (near, 0), (far, 0), (far, KV_PAY))):
        for part in range(2):
            start = base + part * 128
            out[part * GROUP + j * 128 : part * GROUP + (j + 1) * 128] = pay[start : start + 128]


def pair_kernel(first, second, out):
    out[0] = first[...]
    out[1] = second[...]


def masked(block, head):
    lane = lax.broadcasted_iota(jnp.int32, block.shape, 1)
    keep = lane < 64 if head == 0 else lane >= 64
    return jnp.where(keep, block, 0.0).astype(BF16)


def unpack_rows(source, factor, table, stat):
    block = source[0:GROUP].astype(F32) * factor
    for h in range(2):
        table[h] = masked(block, h)
    for j in range(PAIRS):
        pieces = source[GROUP + STAT * j : GROUP + STAT * (j + 1)].astype(F32)
        stat[:, j * LANES : (j + 1) * LANES] = pieces[0:2] + pieces[2:4] + pieces[4:6]


def tile_step(key_tile, value_tile, keys_t, query, grad, logs, spread, dk, dv, dq):
    for h in range(2):
        query_tile, grad_tile = query[h], grad[h]
        scores = dot(key_tile, query_tile, NT) - logs[h : h + 1]
        soft = jnp.exp(scores)
        change = dot(value_tile, grad_tile, NT) - spread[h : h + 1]
        score_grad = (soft * change).astype(BF16)
        dv[...] += dot(soft.astype(BF16), grad_tile, NN)
        dk[...] += dot(score_grad, query_tile, NN)
        head = slice(64 * h, 64 * (h + 1))
        dq[head] += dot(keys_t[head], score_grad, NN)


def turned(block):
    return block.astype(F32).T.astype(BF16)


def attention_kernel(first, count, has_dq, has_dkv, dq_last, dkv_last, qdo, kv, *refs):
    if has_dq:
        dq_in, refs = refs[0], refs[1:]
    if has_dkv:
        dkv_in, refs = refs[0], refs[1:]
    dq_out, dkv_out, keys_t, query, grad, logs, spread, dq, dkv = refs
    for i in range(2):
        unpack_rows(qdo.at[i, 0 : Q_ROWS // 2], 0.125, query.at[i], logs.at[i])
        unpack_rows(qdo.at[i, Q_ROWS // 2 : Q_ROWS], 1.0, grad.at[i], spread.at[i])
    for k in range(first, first + count):
        keys_t[k] = turned(kv[k, 0:GROUP])
    if not dq_last:
        dq = dq_out
    if not dkv_last:
        dkv = dkv_out
    if dq_last or not has_dq:
        dq[...] = dq_in[...] if has_dq else jnp.zeros_like(dq)
    if dkv_last or not has_dkv:
        dkv[...] = dkv_in[...] if has_dkv else jnp.zeros_like(dkv)

    @pl.loop(0, 2 * count)
    def _(step):
        i, k = step % 2, first + step // 2
        tile_step(
            kv[k, 0:GROUP],
            kv[k, GROUP : 2 * GROUP],
            keys_t.at[k],
            query.at[i],
            grad.at[i],
            logs.at[i],
            spread.at[i],
            dkv.at[k, pl.ds(0, GROUP)],
            dkv.at[k, pl.ds(GROUP, GROUP)],
            dq.at[i],
        )

    if dq_last:
        for i in range(2):
            dq_out[i] = (dq[i].T * 0.125).astype(dq_out.dtype)
    if dkv_last:
        dkv_out[...] = dkv[...].astype(dkv_out.dtype)


SLOW = 10**10
MIX = SLOW
JOIN = SLOW
JOIN_KEYS = 1 * 10**9
FORWARD = 0
PAIR = SLOW
WEIGHTS = 0
TILE_FLOPS = 2 * 10 * GROUP * GROUP * 64


def attention(order, name, qdo, kv, dq, dkv, dq_last=None, dkv_last=None, first=0, count=2):
    carry = [a for a in (dq, dkv) if a is not None]
    dq_shape = (2, LANES, GROUP) if dq_last is None else (2, GROUP, LANES)
    aliases = {}
    if dq is not None and dq_last is None:
        aliases[2] = 0
    if dkv is not None and dkv_last is None:
        aliases[1 + len(carry)] = 1
    return order.call(
        functools.partial(
            attention_kernel,
            first,
            count,
            dq is not None,
            dkv is not None,
            dq_last is not None,
            dkv_last is not None,
        ),
        [shaped(dq_shape, dq_last or F32), shaped((2, KV_ROWS, LANES), dkv_last or F32)],
        qdo,
        kv,
        *carry,
        scratch=[
            pltpu.VMEM((2, LANES, GROUP), BF16),
            pltpu.VMEM((2, 2, GROUP, LANES), BF16),
            pltpu.VMEM((2, 2, GROUP, LANES), BF16),
            pltpu.VMEM((2, 2, GROUP), F32),
            pltpu.VMEM((2, 2, GROUP), F32),
            pltpu.VMEM((2, LANES, GROUP), F32),
            pltpu.VMEM((2, KV_ROWS, LANES), F32),
        ],
        aliases=aliases,
        flops=2 * count * TILE_FLOPS,
        name="attention_" + name,
    )


def half_sum_kernel(totals, received, out):
    out[...] = (totals[1].astype(F32) + received[1].astype(F32)).astype(BF16)


def back_kernel(dq, dq_far, dq_near, dkv, dkv_far, dkv_near, keep, near, through, far):
    dq_sum = (dq[0] + dq_far[0].astype(F32) + dq_near[...].astype(F32)).astype(BF16)
    dkv_sum = (dkv[0] + dkv_far[0].astype(F32) + dkv_near[...].astype(F32)).astype(BF16)
    for j, (pay, base) in enumerate(((keep, 0), (near, 0), (through, 0), (far, 0))):
        pay[base : base + 128] = dq_sum[j * 128 : (j + 1) * 128]
        pay[base + 128 : base + 256] = dkv_sum[j * 128 : (j + 1) * 128]
        pay[base + 256 : base + 384] = dkv_sum[GROUP + j * 128 : GROUP + (j + 1) * 128]


def place_kernel(own, near, far, dq, dk, dv):
    me = place_in_group()
    for j, (pay, base) in enumerate(((own, 0), (near, 0), (far, 0), (far, 384))):
        columns = pl.ds(pl.multiple_of((me ^ j) * LANES, LANES), LANES)
        dq[:, columns] = pay[base : base + 128]
        dk[:, columns] = pay[base + 128 : base + 256]
        dv[:, columns] = pay[base + 256 : base + 384]


def turn_kernel(dq, out):
    for i in range(2):
        out[i] = dq[i].T * 0.125


def weights_kernel(source_ref, count_ref, tiles, grad, mix_ref, own, partner, near, crossed, far, keep_ref, send_ref, window, total, left_ref):
    core = lax.axis_index("c")
    window[REACH] = own[...]
    window[jnp.where(core == 0, 4, 2)] = partner[...]
    for block, first in ((near, jnp.where(core == 0, 1, 4)), (crossed, jnp.where(core == 0, 5, 0))):
        window[first] = block[0:128]
        window[first + 1] = block[128:256]
    window[6 * core] = far[...]
    total[...] = jnp.zeros_like(total)
    for e in range(tiles.shape[1]):

        @pl.when(e < count_ref[0])
        def _():
            total[...] += dot(tiles[0, e], window[slot_of(source_ref, e)], NN)

    left_ref[0] = turned(mix_ref[...])
    left_ref[1] = turned(total[...].astype(BF16))

    for out, which in ((keep_ref, core), (send_ref, 1 - core)):
        out[...] = dot(left_ref[which], grad[...], NN).astype(BF16)


def block_rows(distance):
    return pl.ds(pl.multiple_of(lax.rem(ring_place() + distance, 4) * 128, 128), 128)


def core_sum_kernel(keep, received, *outs):
    for k, out in enumerate(outs):
        rows = block_rows(k)
        out[...] = (keep[rows].astype(F32) + received[rows].astype(F32)).astype(out.dtype)


def gather_kernel(*refs):
    for k, block in enumerate(refs[:4]):
        refs[4][block_rows((4 - k) % 4)] = block[...]


def final_kernel(own, other, first, second):
    core = lax.axis_index("c")

    @pl.when(core == 0)
    def _():
        first[...] = own[...].astype(F32)
        second[...] = other[...].astype(F32)

    @pl.when(core == 1)
    def _():
        first[...] = other[...].astype(F32)
        second[...] = own[...].astype(F32)


def add_kernel(*refs):
    total = refs[0][...].astype(F32)
    for ref in refs[1:-1]:
        total = total + ref[...].astype(F32)
    refs[-1][...] = total.astype(BF16)


def add(order, name, *terms):
    (out,) = order.call(add_kernel, [shaped(terms[0].shape)], *terms, name="add_" + name)
    return out


def pair(order, first, second):
    (out,) = order.call(pair_kernel, [shaped((2,) + first.shape)], first, second, flops=PAIR, name="pair")
    return out


def body(
    features,
    queries,
    keys,
    values,
    attn_mix,
    log_sums,
    out_weight,
    msg_weight,
    edge_tiles,
    edge_source,
    edge_count,
    out_grad,
):
    rows, columns = out_grad.shape
    order = Order()
    other_grad = swap(out_grad, "h", 1)
    parts = lax.axis_size(NODE)
    to_near = [(i, (i + (2 if i % 2 == 0 else -2)) % parts) for i in range(parts)]
    to_far = [(i, (i + (-3 if i % 2 == 0 else 3)) % parts) for i in range(parts)]
    partner_features = swap(features, "c", 1)
    far_features = lax.ppermute(features, NODE, to_far)
    arguments = [features, edge_tiles, out_grad, queries, keys, values, log_sums, out_weight, attn_mix, msg_weight]
    arguments = [pltpu.with_memory_space_constraint(a, pltpu.HBM) for a in arguments]
    loaded = order.call(
        functools.partial(load_kernel, len(arguments)),
        [shaped(a.shape, a.dtype) for a in arguments],
        *arguments,
        anywhere=len(arguments),
        scratch=[pltpu.SemaphoreType.DMA((len(arguments),))],
        name="load",
    )
    features, edge_tiles, out_grad, queries, keys, values, log_sums, out_weight, attn_mix, msg_weight = loaded
    wide = (rows, 2 * columns)
    key_pays = order.call(
        pay_kernel, [shaped((KV_PAY, LANES))] * 4, keys, values, name="pay"
    )
    key_near, key_cross = swap(key_pays[1], "c", 1), swap(key_pays[3], "c", 1)
    (near_features,) = order.call(
        chip_kernel, [shaped((2 * rows, columns))], features, partner_features, name="chip"
    )
    near_features = lax.ppermute(near_features, NODE, to_near)
    (key_far,) = order.call(
        forward_kernel, [shaped((2 * KV_PAY, LANES))], key_pays[2], key_cross, name="forward_keys"
    )
    key_far = swap(key_far, "y", 1)
    out_grad, *pays = order.call(
        mix_kernel,
        [shaped(wide)] + [shaped((Q_PAY, LANES))] * 4,
        out_grad,
        other_grad,
        out_weight,
        attn_mix,
        queries,
        log_sums,
        flops=MIX,
        name="mix",
    )
    pay_near, pay_cross = swap(pays[1], "c", 1), swap(pays[3], "c", 1)
    (pay_far,) = order.call(
        forward_kernel, [shaped((2 * Q_PAY, LANES))], pays[2], pay_cross, flops=FORWARD, name="forward"
    )
    pay_far = swap(pay_far, "y", 1)
    (kv,) = order.call(
        join_keys_kernel,
        [shaped((KV_ROWS, LANES))],
        key_pays[0],
        key_near,
        key_far,
        flops=JOIN_KEYS,
        name="join_keys",
    )
    kv_met = meet(kv, "x", 0)
    (qdo,) = order.call(
        join_rows_kernel,
        [shaped((Q_ROWS, LANES))],
        pays[0],
        pay_near,
        pay_far,
        flops=JOIN,
        name="join",
    )
    qdo_met = meet(qdo, "z", 0)
    crossed_features = swap(near_features, "c", 1)
    keep, send = order.call(
        weights_kernel,
        [shaped((columns, 2 * columns)), shaped((columns, 2 * columns))],
        edge_source,
        edge_count,
        edge_tiles,
        out_grad,
        attn_mix,
        features,
        partner_features,
        near_features,
        crossed_features,
        far_features,
        smem=2,
        scratch=[
            pltpu.VMEM((2 * REACH + 1, rows, columns), BF16),
            pltpu.VMEM((rows, columns), F32),
            pltpu.VMEM((2, columns, rows), BF16),
        ],
        flops=WEIGHTS,
        name="weights",
    )
    received = swap(send, "c", 1)
    kv_near = pair(order, kv, kv_met)
    kv_far = meet(kv_near, "x", 1)
    qdo_near = pair(order, qdo, qdo_met)
    qdo_far = meet(qdo_near, "z", 1)
    blocks = order.call(
        core_sum_kernel,
        [shaped(wide, F32)] + [shaped(wide)] * 3,
        keep,
        received,
        name="core_sum",
    )
    blocks = [blocks[0]] + [around(blocks[k], k) for k in range(1, 4)]
    share_send, share_far, share_keep, share_local = order.call(
        share_kernel,
        [
            shaped((3 * rows, columns)),
            shaped((rows, columns)),
            shaped((2 * rows, columns), F32),
            shaped((rows, columns), F32),
        ],
        edge_source,
        edge_count,
        edge_tiles,
        out_grad,
        msg_weight,
        smem=2,
        scratch=[pltpu.VMEM((2 * REACH + 1, rows, columns), F32)],
        name="shares",
    )
    share_received = swap(share_send, "c", 1)
    dq_near, dkv_near = attention(order, "near", qdo_near, kv_near, None, None)
    dq_far, dkv_far = attention(order, "far", qdo_far, kv_far, None, None)
    part = add(order, "ring", *blocks)
    received = across(part, 0)
    share_near, share_local = order.call(
        near_kernel,
        [shaped((2 * rows, columns)), shaped((rows, columns), F32)],
        share_keep,
        share_local,
        share_received,
        name="near",
    )
    share_far, share_near = lax.ppermute(share_far, NODE, to_far), lax.ppermute(share_near, NODE, to_near)
    dq_near, dkv_far = attention(
        order, "far_keys0", qdo_near, kv_far, dq_near, dkv_far, first=0, count=1
    )
    part = add(order, "across0", part, received)
    received = across(part, 1)
    dq_near, dkv_far = attention(
        order, "far_keys1", qdo_near, kv_far, dq_near, dkv_far, None, BF16, first=1, count=1
    )
    dkv_met = meet(dkv_far, "x", 1)
    share_cross, share_local = order.call(
        cross_kernel,
        [shaped((rows, columns)), shaped((rows, columns), F32)],
        share_local,
        share_near,
        share_far,
        flops=SLOW,
        name="cross",
    )
    share_cross = swap(share_cross, "c", 1)
    dq_far, dkv_near = attention(
        order, "far_queries0", qdo_far, kv_near, dq_far, dkv_near, first=0, count=1
    )
    part = add(order, "across1", part, received)
    received = swap(part, "y", 1)
    dq_far, dkv_near = attention(
        order, "far_queries1", qdo_far, kv_near, dq_far, dkv_near, BF16, F32, first=1, count=1
    )
    dq_met = meet(dq_far, "z", 1)
    part = add(order, "y", part, received)
    blocks = [part] + [around(part, k) for k in range(1, 4)]
    (half,) = order.call(
        half_sum_kernel, [shaped((KV_ROWS, LANES))], dkv_near, dkv_met, name="half_dkv"
    )
    dkv_last = meet(half, "x", 0)
    (dq_near,) = order.call(
        turn_kernel, [shaped((2, GROUP, LANES), F32)], dq_near, name="turn"
    )
    (half,) = order.call(half_sum_kernel, [shaped((GROUP, LANES))], dq_near, dq_met, name="half_dq")
    dq_last = meet(half, "z", 0)
    back_own, back_near, back_through, back_cross = order.call(
        back_kernel,
        [shaped((384, LANES))] * 4,
        dq_near,
        dq_met,
        dq_last,
        dkv_near,
        dkv_met,
        dkv_last,
        name="back",
    )
    back_near, back_cross = swap(back_near, "c", 1), swap(back_cross, "c", 1)
    (back_forward,) = order.call(
        forward_kernel, [shaped((768, LANES))], back_through, back_cross, name="forward_back"
    )
    back_far = swap(back_forward, "y", 1)
    (whole,) = order.call(gather_kernel, [shaped((columns, 2 * columns))], *blocks, name="gather")
    received = swap(whole, "c", 1)
    grad_features = add(order, "shares", share_local, share_cross)
    grad_query, grad_key, grad_value = order.call(
        place_kernel, [shaped((rows, columns))] * 3, back_own, back_near, back_far, name="place"
    )
    out_weight_grad, msg_weight_grad = order.call(
        final_kernel,
        [shaped((columns, 2 * columns), F32)] * 2,
        whole,
        received,
        name="final",
    )
    return (grad_features, grad_query, grad_key, grad_value, out_weight_grad, msg_weight_grad)


def solution(mesh):
    fine = Mesh(mesh.devices.reshape(4, 2, 4, 2, 2), NODE + ("h",))
    both = P(NODE, "h")
    placed = (
        both,
        both,
        both,
        both,
        both,
        P("h", NODE),
        P("h", None),
        P("h", None),
        P(NODE, None, None, None),
        P(NODE, None),
        P(NODE),
        both,
    )
    return jax.shard_map(
        body,
        mesh=fine,
        in_specs=placed,
        out_specs=(both, both, both, both, P("h", None), P("h", None)),
        check_vma=False,
    )
```

```python
import functools
import math

import jax
import jax.numpy as jnp
from jax import lax
from jax.experimental import pallas as pl
from jax.experimental.pallas import tpu as pltpu
from jax.sharding import Mesh
from jax.sharding import PartitionSpec as P

BLOCK = 128
REACH = 3
LANES = 128
PAIRS = 4
STAT = 16
GROUP = 512
NODE = ("z", "y", "x", "c")
BF16 = jnp.bfloat16
F32 = jnp.float32
VMEM_LIMIT = 48 * 1024 * 1024

NT = (((1,), (1,)), ((), ()))
NN = (((1,), (0,)), ((), ()))
TN = (((0,), (0,)), ((), ()))


def dot(a, b, dims):
    return lax.dot_general(a, b, dims, preferred_element_type=F32)


def swap(value, axes, mask):
    count = lax.axis_size(axes)
    return lax.ppermute(value, axes, [(i, i ^ mask) for i in range(count)])


NEXT = ((1, 0, 3, 2), (3, 2, 1, 0))


def meet(value, axis, step):
    pairs = [
        (2 * i + core, 2 * NEXT[(step + core) % 2][i] + core) for i in range(4) for core in range(2)
    ]
    return lax.ppermute(value, (axis, "c"), pairs)


def ring_place():
    return jnp.where(lax.axis_index("c") == 0, lax.axis_index("x"), lax.axis_index("z"))


def ring(value, to_first, to_second):
    pairs = []
    for z in range(4):
        for x in range(4):
            pairs.append((8 * z + 2 * x, 8 * to_first[1][z] + 2 * to_first[0][x]))
            pairs.append((8 * z + 2 * x + 1, 8 * to_second[1][z] + 2 * to_second[0][x] + 1))
    return lax.ppermute(value, ("z", "x", "c"), pairs)


STAY = (0, 1, 2, 3)


def around(value, steps):
    turn = tuple((i + steps) % 4 for i in range(4))
    return ring(value, (turn, STAY), (STAY, turn))


def across(value, step):
    return ring(value, (STAY, NEXT[step]), (NEXT[step], STAY))


def place_in_group():
    return lax.axis_index("y") * 2 + lax.axis_index("c")


class Order:
    def __init__(self):
        self.token = None

    def call(self, kernel, outs, *args, scratch=(), smem=0, anywhere=0, aliases={}, flops=0, name=None):
        count, first = len(args), self.token is None
        tokens = [] if first else [self.token]
        results = len(outs)

        def whole(*refs):
            token_out = refs[count + len(tokens) + results]
            token_out[...] = jnp.zeros_like(token_out) if first else refs[count][...]
            outputs = refs[count + len(tokens) : count + len(tokens) + results]
            kernel(*refs[:count], *outputs, *refs[count + len(tokens) + results + 1 :])

        specs = [pl.BlockSpec(memory_space=pltpu.SMEM)] * smem
        specs += [pl.BlockSpec(memory_space=pltpu.HBM)] * anywhere
        specs += [pl.BlockSpec(memory_space=pltpu.VMEM)] * (count - smem - anywhere + len(tokens))
        size = sum(math.prod(a.shape) * a.dtype.itemsize for a in (*args, *outs))
        *values, self.token = pl.pallas_call(
            whole,
            out_shape=[*outs, shaped((8, LANES), F32)],
            in_specs=specs,
            out_specs=[pl.BlockSpec(memory_space=pltpu.VMEM)] * (results + 1),
            scratch_shapes=list(scratch),
            input_output_aliases=aliases,
            cost_estimate=pl.CostEstimate(flops=flops, bytes_accessed=size, transcendentals=0),
            compiler_params=pltpu.CompilerParams(vmem_limit_bytes=VMEM_LIMIT),
            name=name,
        )(*args, *tokens)
        return values


def shaped(shape, dtype=BF16):
    return jax.ShapeDtypeStruct(shape, dtype)


def three_pieces(value):
    high = value.astype(BF16)
    rest = value - high.astype(F32)
    middle = rest.astype(BF16)
    low = (rest - middle.astype(F32)).astype(BF16)
    return jnp.concatenate(
        [high.astype(F32), middle.astype(F32), low.astype(F32), jnp.zeros((STAT - 6, LANES), F32)],
        axis=0,
    ).astype(BF16)


def pair_rows(table, pair):
    rows = table[0:2]
    for other in range(1, PAIRS):
        rows = jnp.where(pair == other, table[2 * other : 2 * other + 2], rows)
    return rows


Q_PAY = 288
KV_PAY = 256
Q_ROWS = 2 * (GROUP + PAIRS * STAT)
KV_ROWS = 2 * GROUP


def load_kernel(count, *refs):
    sem = refs[-1]
    copies = [
        pltpu.make_async_copy(source, target, sem.at[i])
        for i, (source, target) in enumerate(zip(refs[:count], refs[count : 2 * count]))
    ]
    for copy in copies:
        copy.start()
    for copy in copies:
        copy.wait()


def whole_rows(own, other, out):
    side, half = lax.axis_index("h"), own.shape[1]
    out[:, pl.ds(pl.multiple_of(side * half, half), half)] = own[...]
    out[:, pl.ds(pl.multiple_of((1 - side) * half, half), half)] = other[...]


def slot_of(source_ref, e):
    parts = lax.axis_size(NODE)
    distance = lax.rem(source_ref[0, e] - lax.axis_index(NODE) + REACH + 2 * parts, parts)
    return jnp.clip(distance, 0, 2 * REACH)


def chip_kernel(own, other, out):
    core = lax.axis_index("c")
    out[pl.ds(pl.multiple_of(core * 128, 128), 128)] = own[...]
    out[pl.ds(pl.multiple_of((1 - core) * 128, 128), 128)] = other[...]


def share_kernel(source_ref, count_ref, tiles, grad, weight, send, far, keep, local, total):
    total[...] = jnp.zeros_like(total)
    grad_aggregate = dot(grad[...], weight[...], NT).astype(BF16)
    for e in range(tiles.shape[1]):

        @pl.when(e < count_ref[0])
        def _():
            total[slot_of(source_ref, e)] += dot(tiles[0, e], grad_aggregate, TN)

    core = lax.axis_index("c")

    def share(on_first, on_second):
        return total[jnp.where(core == 0, on_first + REACH, on_second + REACH)]

    for i, (on_first, on_second) in enumerate(((-2, 1), (-1, 2), (1, -1))):
        send[i * 128 : (i + 1) * 128] = share(on_first, on_second).astype(BF16)
    for i, (on_first, on_second) in enumerate(((2, -3), (3, -2))):
        keep[i * 128 : (i + 1) * 128] = share(on_first, on_second)
    far[...] = share(-3, 3).astype(BF16)
    local[...] = total[REACH]


def near_kernel(keep, local, received, near, local_out):
    near[...] = (keep[...] + received[0:256].astype(F32)).astype(BF16)
    local_out[...] = local[...] + received[256:384].astype(F32)


def cross_kernel(local, near, far, send, local_out):
    core = lax.axis_index("c")
    mine = pl.ds(pl.multiple_of(core * 128, 128), 128)
    other = pl.ds(pl.multiple_of((1 - core) * 128, 128), 128)
    send[...] = near[other]
    local_out[...] = local[...] + near[mine].astype(F32) + far[...].astype(F32)


def pay_kernel(k_ref, v_ref, *pays):
    me = place_in_group()
    for j, pay in enumerate(pays):
        columns = pl.ds(pl.multiple_of((me ^ j) * LANES, LANES), LANES)
        pay[0:128] = k_ref[:, columns]
        pay[128:256] = v_ref[:, columns]


def mix_kernel(own, other, weight_ref, mix_ref, q_ref, log_ref, whole, *pays):
    whole_rows(own, other, whole)
    grad = dot(whole[...], weight_ref[...], NT).astype(BF16)
    product = grad.astype(F32) * mix_ref[...].astype(F32)
    turned_product = product.T
    rows = [jnp.sum(turned_product[64 * i : 64 * (i + 1)], axis=0, keepdims=True) for i in range(8)]
    spread = jnp.concatenate(rows, axis=0)
    logs = log_ref[...]
    me = place_in_group()
    for j, pay in enumerate(pays):
        pair = me ^ j
        columns = pl.ds(pl.multiple_of(pair * LANES, LANES), LANES)
        block = grad[:, 0:LANES]
        for other in range(1, PAIRS):
            block = jnp.where(pair == other, grad[:, other * LANES : (other + 1) * LANES], block)
        pay[0:128] = q_ref[:, columns]
        pay[128:144] = three_pieces(pair_rows(logs, pair))
        pay[144:272] = block
        pay[272:288] = three_pieces(pair_rows(spread, pair))


def forward_kernel(own, received, out):
    rows = own.shape[0]
    out[0:rows] = own[...]
    out[rows : 2 * rows] = received[...]


def join_rows_kernel(own, near, far, out):
    for j, (pay, base) in enumerate(((own, 0), (near, 0), (far, 0), (far, Q_PAY))):
        for part in range(2):
            at, start = part * (Q_ROWS // 2), base + part * 144
            out[at + j * 128 : at + (j + 1) * 128] = pay[start : start + 128]
            stats = at + GROUP + j * STAT
            out[stats : stats + STAT] = pay[start + 128 : start + 144]


def join_keys_kernel(own, near, far, out):
    for j, (pay, base) in enumerate(((own, 0), (near, 0), (far, 0), (far, KV_PAY))):
        for part in range(2):
            start = base + part * 128
            out[part * GROUP + j * 128 : part * GROUP + (j + 1) * 128] = pay[start : start + 128]


def pair_kernel(first, second, out):
    out[0] = first[...]
    out[1] = second[...]


def masked(block, head):
    lane = lax.broadcasted_iota(jnp.int32, block.shape, 1)
    keep = lane < 64 if head == 0 else lane >= 64
    return jnp.where(keep, block, 0.0).astype(BF16)


def unpack_rows(source, factor, table, stat):
    block = source[0:GROUP].astype(F32) * factor
    for h in range(2):
        table[h] = masked(block, h)
    for j in range(PAIRS):
        pieces = source[GROUP + STAT * j : GROUP + STAT * (j + 1)].astype(F32)
        stat[:, j * LANES : (j + 1) * LANES] = pieces[0:2] + pieces[2:4] + pieces[4:6]


def tile_step(key_tile, value_tile, keys_t, query, grad, logs, spread, dk, dv, dq):
    for h in range(2):
        query_tile, grad_tile = query[h], grad[h]
        scores = dot(key_tile, query_tile, NT) - logs[h : h + 1]
        soft = jnp.exp(scores)
        change = dot(value_tile, grad_tile, NT) - spread[h : h + 1]
        score_grad = (soft * change).astype(BF16)
        dv[...] += dot(soft.astype(BF16), grad_tile, NN)
        dk[...] += dot(score_grad, query_tile, NN)
        head = slice(64 * h, 64 * (h + 1))
        dq[head] += dot(keys_t[head], score_grad, NN)


def turned(block):
    return block.astype(F32).T.astype(BF16)


def attention_kernel(first, count, has_dq, has_dkv, dq_last, dkv_last, qdo, kv, *refs):
    if has_dq:
        dq_in, refs = refs[0], refs[1:]
    if has_dkv:
        dkv_in, refs = refs[0], refs[1:]
    dq_out, dkv_out, keys_t, query, grad, logs, spread, dq, dkv = refs
    for i in range(2):
        unpack_rows(qdo.at[i, 0 : Q_ROWS // 2], 0.125, query.at[i], logs.at[i])
        unpack_rows(qdo.at[i, Q_ROWS // 2 : Q_ROWS], 1.0, grad.at[i], spread.at[i])
    for k in range(first, first + count):
        keys_t[k] = turned(kv[k, 0:GROUP])
    if not dq_last:
        dq = dq_out
    if not dkv_last:
        dkv = dkv_out
    if dq_last or not has_dq:
        dq[...] = dq_in[...] if has_dq else jnp.zeros_like(dq)
    if dkv_last or not has_dkv:
        dkv[...] = dkv_in[...] if has_dkv else jnp.zeros_like(dkv)

    @pl.loop(0, 2 * count)
    def _(step):
        i, k = step % 2, first + step // 2
        tile_step(
            kv[k, 0:GROUP],
            kv[k, GROUP : 2 * GROUP],
            keys_t.at[k],
            query.at[i],
            grad.at[i],
            logs.at[i],
            spread.at[i],
            dkv.at[k, pl.ds(0, GROUP)],
            dkv.at[k, pl.ds(GROUP, GROUP)],
            dq.at[i],
        )

    if dq_last:
        for i in range(2):
            dq_out[i] = (dq[i].T * 0.125).astype(dq_out.dtype)
    if dkv_last:
        dkv_out[...] = dkv[...].astype(dkv_out.dtype)


SLOW = 10**10
MIX = SLOW
JOIN = SLOW
JOIN_KEYS = 1 * 10**9
FORWARD = 0
PAIR = SLOW
WEIGHTS = 0
TILE_FLOPS = 2 * 10 * GROUP * GROUP * 64


def attention(order, name, qdo, kv, dq, dkv, dq_last=None, dkv_last=None, first=0, count=2):
    carry = [a for a in (dq, dkv) if a is not None]
    dq_shape = (2, LANES, GROUP) if dq_last is None else (2, GROUP, LANES)
    aliases = {}
    if dq is not None and dq_last is None:
        aliases[2] = 0
    if dkv is not None and dkv_last is None:
        aliases[1 + len(carry)] = 1
    return order.call(
        functools.partial(
            attention_kernel,
            first,
            count,
            dq is not None,
            dkv is not None,
            dq_last is not None,
            dkv_last is not None,
        ),
        [shaped(dq_shape, dq_last or F32), shaped((2, KV_ROWS, LANES), dkv_last or F32)],
        qdo,
        kv,
        *carry,
        scratch=[
            pltpu.VMEM((2, LANES, GROUP), BF16),
            pltpu.VMEM((2, 2, GROUP, LANES), BF16),
            pltpu.VMEM((2, 2, GROUP, LANES), BF16),
            pltpu.VMEM((2, 2, GROUP), F32),
            pltpu.VMEM((2, 2, GROUP), F32),
            pltpu.VMEM((2, LANES, GROUP), F32),
            pltpu.VMEM((2, KV_ROWS, LANES), F32),
        ],
        aliases=aliases,
        flops=2 * count * TILE_FLOPS,
        name="attention_" + name,
    )


def half_sum_kernel(totals, received, out):
    out[...] = (totals[1].astype(F32) + received[1].astype(F32)).astype(BF16)


def back_kernel(dq, dq_far, dq_near, dkv, dkv_far, dkv_near, keep, near, through, far):
    dq_sum = (dq[0] + dq_far[0].astype(F32) + dq_near[...].astype(F32)).astype(BF16)
    dkv_sum = (dkv[0] + dkv_far[0].astype(F32) + dkv_near[...].astype(F32)).astype(BF16)
    for j, (pay, base) in enumerate(((keep, 0), (near, 0), (through, 0), (far, 0))):
        pay[base : base + 128] = dq_sum[j * 128 : (j + 1) * 128]
        pay[base + 128 : base + 256] = dkv_sum[j * 128 : (j + 1) * 128]
        pay[base + 256 : base + 384] = dkv_sum[GROUP + j * 128 : GROUP + (j + 1) * 128]


def place_kernel(own, near, far, dq, dk, dv):
    me = place_in_group()
    for j, (pay, base) in enumerate(((own, 0), (near, 0), (far, 0), (far, 384))):
        columns = pl.ds(pl.multiple_of((me ^ j) * LANES, LANES), LANES)
        dq[:, columns] = pay[base : base + 128]
        dk[:, columns] = pay[base + 128 : base + 256]
        dv[:, columns] = pay[base + 256 : base + 384]


def turn_kernel(dq, out):
    for i in range(2):
        out[i] = dq[i].T * 0.125


def weights_kernel(source_ref, count_ref, tiles, grad, mix_ref, own, partner, near, crossed, far, keep_ref, send_ref, window, total, left_ref):
    core = lax.axis_index("c")
    window[REACH] = own[...]
    window[jnp.where(core == 0, 4, 2)] = partner[...]
    for block, first in ((near, jnp.where(core == 0, 1, 4)), (crossed, jnp.where(core == 0, 5, 0))):
        window[first] = block[0:128]
        window[first + 1] = block[128:256]
    window[6 * core] = far[...]
    total[...] = jnp.zeros_like(total)
    for e in range(tiles.shape[1]):

        @pl.when(e < count_ref[0])
        def _():
            total[...] += dot(tiles[0, e], window[slot_of(source_ref, e)], NN)

    left_ref[0] = turned(mix_ref[...])
    left_ref[1] = turned(total[...].astype(BF16))

    for out, which in ((keep_ref, core), (send_ref, 1 - core)):
        out[...] = dot(left_ref[which], grad[...], NN).astype(BF16)


def block_rows(distance):
    return pl.ds(pl.multiple_of(lax.rem(ring_place() + distance, 4) * 128, 128), 128)


def core_sum_kernel(keep, received, *outs):
    for k, out in enumerate(outs):
        rows = block_rows(k)
        out[...] = (keep[rows].astype(F32) + received[rows].astype(F32)).astype(out.dtype)


def gather_kernel(*refs):
    for k, block in enumerate(refs[:4]):
        refs[4][block_rows((4 - k) % 4)] = block[...]


def final_kernel(own, other, first, second):
    core = lax.axis_index("c")

    @pl.when(core == 0)
    def _():
        first[...] = own[...].astype(F32)
        second[...] = other[...].astype(F32)

    @pl.when(core == 1)
    def _():
        first[...] = other[...].astype(F32)
        second[...] = own[...].astype(F32)


def add_kernel(*refs):
    total = refs[0][...].astype(F32)
    for ref in refs[1:-1]:
        total = total + ref[...].astype(F32)
    refs[-1][...] = total.astype(BF16)


def add(order, name, *terms):
    (out,) = order.call(add_kernel, [shaped(terms[0].shape)], *terms, name="add_" + name)
    return out


def pair(order, first, second):
    (out,) = order.call(pair_kernel, [shaped((2,) + first.shape)], first, second, flops=PAIR, name="pair")
    return out


def body(
    features,
    queries,
    keys,
    values,
    attn_mix,
    log_sums,
    out_weight,
    msg_weight,
    edge_tiles,
    edge_source,
    edge_count,
    out_grad,
):
    rows, columns = out_grad.shape
    order = Order()
    other_grad = swap(out_grad, "h", 1)
    parts = lax.axis_size(NODE)
    to_near = [(i, (i + (2 if i % 2 == 0 else -2)) % parts) for i in range(parts)]
    to_far = [(i, (i + (-3 if i % 2 == 0 else 3)) % parts) for i in range(parts)]
    partner_features = swap(features, "c", 1)
    far_features = lax.ppermute(features, NODE, to_far)
    arguments = [features, edge_tiles, out_grad, queries, keys, values, log_sums, out_weight, attn_mix, msg_weight]
    arguments = [pltpu.with_memory_space_constraint(a, pltpu.HBM) for a in arguments]
    loaded = order.call(
        functools.partial(load_kernel, len(arguments)),
        [shaped(a.shape, a.dtype) for a in arguments],
        *arguments,
        anywhere=len(arguments),
        scratch=[pltpu.SemaphoreType.DMA((len(arguments),))],
        name="load",
    )
    features, edge_tiles, out_grad, queries, keys, values, log_sums, out_weight, attn_mix, msg_weight = loaded
    wide = (rows, 2 * columns)
    key_pays = order.call(
        pay_kernel, [shaped((KV_PAY, LANES))] * 4, keys, values, name="pay"
    )
    key_near, key_cross = swap(key_pays[1], "c", 1), swap(key_pays[3], "c", 1)
    (near_features,) = order.call(
        chip_kernel, [shaped((2 * rows, columns))], features, partner_features, name="chip"
    )
    near_features = lax.ppermute(near_features, NODE, to_near)
    (key_far,) = order.call(
        forward_kernel, [shaped((2 * KV_PAY, LANES))], key_pays[2], key_cross, name="forward_keys"
    )
    key_far = swap(key_far, "y", 1)
    out_grad, *pays = order.call(
        mix_kernel,
        [shaped(wide)] + [shaped((Q_PAY, LANES))] * 4,
        out_grad,
        other_grad,
        out_weight,
        attn_mix,
        queries,
        log_sums,
        flops=MIX,
        name="mix",
    )
    pay_near, pay_cross = swap(pays[1], "c", 1), swap(pays[3], "c", 1)
    (pay_far,) = order.call(
        forward_kernel, [shaped((2 * Q_PAY, LANES))], pays[2], pay_cross, flops=FORWARD, name="forward"
    )
    pay_far = swap(pay_far, "y", 1)
    (kv,) = order.call(
        join_keys_kernel,
        [shaped((KV_ROWS, LANES))],
        key_pays[0],
        key_near,
        key_far,
        flops=JOIN_KEYS,
        name="join_keys",
    )
    kv_met = meet(kv, "x", 0)
    (qdo,) = order.call(
        join_rows_kernel,
        [shaped((Q_ROWS, LANES))],
        pays[0],
        pay_near,
        pay_far,
        flops=JOIN,
        name="join",
    )
    qdo_met = meet(qdo, "z", 0)
    crossed_features = swap(near_features, "c", 1)
    keep, send = order.call(
        weights_kernel,
        [shaped((columns, 2 * columns)), shaped((columns, 2 * columns))],
        edge_source,
        edge_count,
        edge_tiles,
        out_grad,
        attn_mix,
        features,
        partner_features,
        near_features,
        crossed_features,
        far_features,
        smem=2,
        scratch=[
            pltpu.VMEM((2 * REACH + 1, rows, columns), BF16),
            pltpu.VMEM((rows, columns), F32),
            pltpu.VMEM((2, columns, rows), BF16),
        ],
        flops=WEIGHTS,
        name="weights",
    )
    received = swap(send, "c", 1)
    kv_near = pair(order, kv, kv_met)
    kv_far = meet(kv_near, "x", 1)
    qdo_near = pair(order, qdo, qdo_met)
    qdo_far = meet(qdo_near, "z", 1)
    blocks = order.call(
        core_sum_kernel,
        [shaped(wide, F32)] + [shaped(wide)] * 3,
        keep,
        received,
        name="core_sum",
    )
    blocks = [blocks[0]] + [around(blocks[k], k) for k in range(1, 4)]
    share_send, share_far, share_keep, share_local = order.call(
        share_kernel,
        [
            shaped((3 * rows, columns)),
            shaped((rows, columns)),
            shaped((2 * rows, columns), F32),
            shaped((rows, columns), F32),
        ],
        edge_source,
        edge_count,
        edge_tiles,
        out_grad,
        msg_weight,
        smem=2,
        scratch=[pltpu.VMEM((2 * REACH + 1, rows, columns), F32)],
        name="shares",
    )
    share_received = swap(share_send, "c", 1)
    dq_near, dkv_near = attention(order, "near", qdo_near, kv_near, None, None)
    share_near, share_local = order.call(
        near_kernel,
        [shaped((2 * rows, columns)), shaped((rows, columns), F32)],
        share_keep,
        share_local,
        share_received,
        name="near",
    )
    share_far, share_near = lax.ppermute(share_far, NODE, to_far), lax.ppermute(share_near, NODE, to_near)
    dq_far, dkv_far = attention(order, "far", qdo_far, kv_far, None, None)
    part = add(order, "ring", *blocks)
    received = across(part, 0)
    share_cross, share_local = order.call(
        cross_kernel,
        [shaped((rows, columns)), shaped((rows, columns), F32)],
        share_local,
        share_near,
        share_far,
        flops=SLOW,
        name="cross",
    )
    share_cross = swap(share_cross, "c", 1)
    dq_near, dkv_far = attention(
        order, "far_keys0", qdo_near, kv_far, dq_near, dkv_far, first=0, count=1
    )
    part = add(order, "across0", part, received)
    received = across(part, 1)
    dq_near, dkv_far = attention(
        order, "far_keys1", qdo_near, kv_far, dq_near, dkv_far, None, BF16, first=1, count=1
    )
    dkv_met = meet(dkv_far, "x", 1)
    dq_far, dkv_near = attention(
        order, "far_queries0", qdo_far, kv_near, dq_far, dkv_near, first=0, count=1
    )
    part = add(order, "across1", part, received)
    received = swap(part, "y", 1)
    dq_far, dkv_near = attention(
        order, "far_queries1", qdo_far, kv_near, dq_far, dkv_near, BF16, F32, first=1, count=1
    )
    dq_met = meet(dq_far, "z", 1)
    part = add(order, "y", part, received)
    blocks = [part] + [around(part, k) for k in range(1, 4)]
    (half,) = order.call(
        half_sum_kernel, [shaped((KV_ROWS, LANES))], dkv_near, dkv_met, name="half_dkv"
    )
    dkv_last = meet(half, "x", 0)
    (dq_near,) = order.call(
        turn_kernel, [shaped((2, GROUP, LANES), F32)], dq_near, name="turn"
    )
    (half,) = order.call(half_sum_kernel, [shaped((GROUP, LANES))], dq_near, dq_met, name="half_dq")
    dq_last = meet(half, "z", 0)
    back_own, back_near, back_through, back_cross = order.call(
        back_kernel,
        [shaped((384, LANES))] * 4,
        dq_near,
        dq_met,
        dq_last,
        dkv_near,
        dkv_met,
        dkv_last,
        name="back",
    )
    back_near, back_cross = swap(back_near, "c", 1), swap(back_cross, "c", 1)
    (back_forward,) = order.call(
        forward_kernel, [shaped((768, LANES))], back_through, back_cross, name="forward_back"
    )
    back_far = swap(back_forward, "y", 1)
    (whole,) = order.call(gather_kernel, [shaped((columns, 2 * columns))], *blocks, name="gather")
    received = swap(whole, "c", 1)
    grad_features = add(order, "shares", share_local, share_cross)
    grad_query, grad_key, grad_value = order.call(
        place_kernel, [shaped((rows, columns))] * 3, back_own, back_near, back_far, name="place"
    )
    out_weight_grad, msg_weight_grad = order.call(
        final_kernel,
        [shaped((columns, 2 * columns), F32)] * 2,
        whole,
        received,
        name="final",
    )
    return (grad_features, grad_query, grad_key, grad_value, out_weight_grad, msg_weight_grad)


def solution(mesh):
    fine = Mesh(mesh.devices.reshape(4, 2, 4, 2, 2), NODE + ("h",))
    both = P(NODE, "h")
    placed = (
        both,
        both,
        both,
        both,
        both,
        P("h", NODE),
        P("h", None),
        P("h", None),
        P(NODE, None, None, None),
        P(NODE, None),
        P(NODE),
        both,
    )
    return jax.shard_map(
        body,
        mesh=fine,
        in_specs=placed,
        out_specs=(both, both, both, both, P("h", None), P("h", None)),
        check_vma=False,
    )
```

```python
import functools
import math

import jax
import jax.numpy as jnp
from jax import lax
from jax.experimental import pallas as pl
from jax.experimental.pallas import tpu as pltpu
from jax.sharding import Mesh
from jax.sharding import PartitionSpec as P

BLOCK = 128
REACH = 3
LANES = 128
PAIRS = 4
STAT = 16
GROUP = 512
NODE = ("z", "y", "x", "c")
BF16 = jnp.bfloat16
F32 = jnp.float32
VMEM_LIMIT = 48 * 1024 * 1024

NT = (((1,), (1,)), ((), ()))
NN = (((1,), (0,)), ((), ()))
TN = (((0,), (0,)), ((), ()))


def dot(a, b, dims):
    return lax.dot_general(a, b, dims, preferred_element_type=F32)


def swap(value, axes, mask):
    count = lax.axis_size(axes)
    return lax.ppermute(value, axes, [(i, i ^ mask) for i in range(count)])


NEXT = ((1, 0, 3, 2), (3, 2, 1, 0))


def meet(value, axis, step):
    pairs = [
        (2 * i + core, 2 * NEXT[(step + core) % 2][i] + core) for i in range(4) for core in range(2)
    ]
    return lax.ppermute(value, (axis, "c"), pairs)


def ring_place():
    return jnp.where(lax.axis_index("c") == 0, lax.axis_index("x"), lax.axis_index("z"))


def ring(value, to_first, to_second):
    pairs = []
    for z in range(4):
        for x in range(4):
            pairs.append((8 * z + 2 * x, 8 * to_first[1][z] + 2 * to_first[0][x]))
            pairs.append((8 * z + 2 * x + 1, 8 * to_second[1][z] + 2 * to_second[0][x] + 1))
    return lax.ppermute(value, ("z", "x", "c"), pairs)


STAY = (0, 1, 2, 3)


def around(value, steps):
    turn = tuple((i + steps) % 4 for i in range(4))
    return ring(value, (turn, STAY), (STAY, turn))


def across(value, step):
    return ring(value, (STAY, NEXT[step]), (NEXT[step], STAY))


def place_in_group():
    return lax.axis_index("y") * 2 + lax.axis_index("c")


class Order:
    def __init__(self):
        self.token = None

    def call(self, kernel, outs, *args, scratch=(), smem=0, anywhere=0, aliases={}, flops=0, name=None):
        count, first = len(args), self.token is None
        tokens = [] if first else [self.token]
        results = len(outs)

        def whole(*refs):
            token_out = refs[count + len(tokens) + results]
            token_out[...] = jnp.zeros_like(token_out) if first else refs[count][...]
            outputs = refs[count + len(tokens) : count + len(tokens) + results]
            kernel(*refs[:count], *outputs, *refs[count + len(tokens) + results + 1 :])

        specs = [pl.BlockSpec(memory_space=pltpu.SMEM)] * smem
        specs += [pl.BlockSpec(memory_space=pltpu.HBM)] * anywhere
        specs += [pl.BlockSpec(memory_space=pltpu.VMEM)] * (count - smem - anywhere + len(tokens))
        size = sum(math.prod(a.shape) * a.dtype.itemsize for a in (*args, *outs))
        *values, self.token = pl.pallas_call(
            whole,
            out_shape=[*outs, shaped((8, LANES), F32)],
            in_specs=specs,
            out_specs=[pl.BlockSpec(memory_space=pltpu.VMEM)] * (results + 1),
            scratch_shapes=list(scratch),
            input_output_aliases=aliases,
            cost_estimate=pl.CostEstimate(flops=flops, bytes_accessed=size, transcendentals=0),
            compiler_params=pltpu.CompilerParams(vmem_limit_bytes=VMEM_LIMIT),
            name=name,
        )(*args, *tokens)
        return values


def shaped(shape, dtype=BF16):
    return jax.ShapeDtypeStruct(shape, dtype)


def three_pieces(value):
    high = value.astype(BF16)
    rest = value - high.astype(F32)
    middle = rest.astype(BF16)
    low = (rest - middle.astype(F32)).astype(BF16)
    return jnp.concatenate(
        [high.astype(F32), middle.astype(F32), low.astype(F32), jnp.zeros((STAT - 6, LANES), F32)],
        axis=0,
    ).astype(BF16)


def pair_rows(table, pair):
    rows = table[0:2]
    for other in range(1, PAIRS):
        rows = jnp.where(pair == other, table[2 * other : 2 * other + 2], rows)
    return rows


Q_PAY = 288
KV_PAY = 256
Q_ROWS = 2 * (GROUP + PAIRS * STAT)
KV_ROWS = 2 * GROUP


def load_kernel(count, *refs):
    sem = refs[-1]
    copies = [
        pltpu.make_async_copy(source, target, sem.at[i])
        for i, (source, target) in enumerate(zip(refs[:count], refs[count : 2 * count]))
    ]
    for copy in copies:
        copy.start()
    for copy in copies:
        copy.wait()


def whole_rows(own, other, out):
    side, half = lax.axis_index("h"), own.shape[1]
    out[:, pl.ds(pl.multiple_of(side * half, half), half)] = own[...]
    out[:, pl.ds(pl.multiple_of((1 - side) * half, half), half)] = other[...]


def slot_of(source_ref, e):
    parts = lax.axis_size(NODE)
    distance = lax.rem(source_ref[0, e] - lax.axis_index(NODE) + REACH + 2 * parts, parts)
    return jnp.clip(distance, 0, 2 * REACH)


def chip_kernel(own, other, out):
    core = lax.axis_index("c")
    out[pl.ds(pl.multiple_of(core * 128, 128), 128)] = own[...]
    out[pl.ds(pl.multiple_of((1 - core) * 128, 128), 128)] = other[...]


def share_kernel(source_ref, count_ref, tiles, grad, weight, send, far, keep, local, total):
    total[...] = jnp.zeros_like(total)
    grad_aggregate = dot(grad[...], weight[...], NT).astype(BF16)
    for e in range(tiles.shape[1]):

        @pl.when(e < count_ref[0])
        def _():
            total[slot_of(source_ref, e)] += dot(tiles[0, e], grad_aggregate, TN)

    core = lax.axis_index("c")

    def share(on_first, on_second):
        return total[jnp.where(core == 0, on_first + REACH, on_second + REACH)]

    for i, (on_first, on_second) in enumerate(((-2, 1), (-1, 2), (1, -1))):
        send[i * 128 : (i + 1) * 128] = share(on_first, on_second).astype(BF16)
    for i, (on_first, on_second) in enumerate(((2, -3), (3, -2))):
        keep[i * 128 : (i + 1) * 128] = share(on_first, on_second)
    far[...] = share(-3, 3).astype(BF16)
    local[...] = total[REACH]


def near_kernel(keep, local, received, near, local_out):
    near[...] = (keep[...] + received[0:256].astype(F32)).astype(BF16)
    local_out[...] = local[...] + received[256:384].astype(F32)


def cross_kernel(local, near, far, send, local_out):
    core = lax.axis_index("c")
    mine = pl.ds(pl.multiple_of(core * 128, 128), 128)
    other = pl.ds(pl.multiple_of((1 - core) * 128, 128), 128)
    send[...] = near[other]
    local_out[...] = local[...] + near[mine].astype(F32) + far[...].astype(F32)


def pay_kernel(k_ref, v_ref, *pays):
    me = place_in_group()
    for j, pay in enumerate(pays):
        columns = pl.ds(pl.multiple_of((me ^ j) * LANES, LANES), LANES)
        pay[0:128] = k_ref[:, columns]
        pay[128:256] = v_ref[:, columns]


def mix_kernel(own, other, weight_ref, mix_ref, q_ref, log_ref, whole, *pays):
    whole_rows(own, other, whole)
    grad = dot(whole[...], weight_ref[...], NT).astype(BF16)
    product = grad.astype(F32) * mix_ref[...].astype(F32)
    turned_product = product.T
    rows = [jnp.sum(turned_product[64 * i : 64 * (i + 1)], axis=0, keepdims=True) for i in range(8)]
    spread = jnp.concatenate(rows, axis=0)
    logs = log_ref[...]
    me = place_in_group()
    for j, pay in enumerate(pays):
        pair = me ^ j
        columns = pl.ds(pl.multiple_of(pair * LANES, LANES), LANES)
        block = grad[:, 0:LANES]
        for other in range(1, PAIRS):
            block = jnp.where(pair == other, grad[:, other * LANES : (other + 1) * LANES], block)
        pay[0:128] = q_ref[:, columns]
        pay[128:144] = three_pieces(pair_rows(logs, pair))
        pay[144:272] = block
        pay[272:288] = three_pieces(pair_rows(spread, pair))


def forward_kernel(own, received, out):
    rows = own.shape[0]
    out[0:rows] = own[...]
    out[rows : 2 * rows] = received[...]


def join_rows_kernel(own, near, far, out):
    for j, (pay, base) in enumerate(((own, 0), (near, 0), (far, 0), (far, Q_PAY))):
        for part in range(2):
            at, start = part * (Q_ROWS // 2), base + part * 144
            out[at + j * 128 : at + (j + 1) * 128] = pay[start : start + 128]
            stats = at + GROUP + j * STAT
            out[stats : stats + STAT] = pay[start + 128 : start + 144]


def join_keys_kernel(own, near, far, out):
    for j, (pay, base) in enumerate(((own, 0), (near, 0), (far, 0), (far, KV_PAY))):
        for part in range(2):
            start = base + part * 128
            out[part * GROUP + j * 128 : part * GROUP + (j + 1) * 128] = pay[start : start + 128]


def pair_kernel(first, second, out):
    out[0] = first[...]
    out[1] = second[...]


def masked(block, head):
    lane = lax.broadcasted_iota(jnp.int32, block.shape, 1)
    keep = lane < 64 if head == 0 else lane >= 64
    return jnp.where(keep, block, 0.0).astype(BF16)


def unpack_rows(source, factor, table, stat):
    block = source[0:GROUP].astype(F32) * factor
    for h in range(2):
        table[h] = masked(block, h)
    for j in range(PAIRS):
        pieces = source[GROUP + STAT * j : GROUP + STAT * (j + 1)].astype(F32)
        stat[:, j * LANES : (j + 1) * LANES] = pieces[0:2] + pieces[2:4] + pieces[4:6]


def tile_step(key_tile, value_tile, keys_t, query, grad, logs, spread, dk, dv, dq):
    for h in range(2):
        query_tile, grad_tile = query[h], grad[h]
        scores = dot(key_tile, query_tile, NT) - logs[h : h + 1]
        soft = jnp.exp(scores)
        change = dot(value_tile, grad_tile, NT) - spread[h : h + 1]
        score_grad = (soft * change).astype(BF16)
        dv[...] += dot(soft.astype(BF16), grad_tile, NN)
        dk[...] += dot(score_grad, query_tile, NN)
        head = slice(64 * h, 64 * (h + 1))
        dq[head] += dot(keys_t[head], score_grad, NN)


def turned(block):
    return block.astype(F32).T.astype(BF16)


def attention_kernel(first, count, has_dq, has_dkv, dq_last, dkv_last, qdo, kv, *refs):
    if has_dq:
        dq_in, refs = refs[0], refs[1:]
    if has_dkv:
        dkv_in, refs = refs[0], refs[1:]
    dq_out, dkv_out, keys_t, query, grad, logs, spread, dq, dkv = refs
    for i in range(2):
        unpack_rows(qdo.at[i, 0 : Q_ROWS // 2], 0.125, query.at[i], logs.at[i])
        unpack_rows(qdo.at[i, Q_ROWS // 2 : Q_ROWS], 1.0, grad.at[i], spread.at[i])
    for k in range(first, first + count):
        keys_t[k] = turned(kv[k, 0:GROUP])
    if not dq_last:
        dq = dq_out
    if not dkv_last:
        dkv = dkv_out
    if dq_last or not has_dq:
        dq[...] = dq_in[...] if has_dq else jnp.zeros_like(dq)
    if dkv_last or not has_dkv:
        dkv[...] = dkv_in[...] if has_dkv else jnp.zeros_like(dkv)

    @pl.loop(0, 2 * count)
    def _(step):
        i, k = step % 2, first + step // 2
        tile_step(
            kv[k, 0:GROUP],
            kv[k, GROUP : 2 * GROUP],
            keys_t.at[k],
            query.at[i],
            grad.at[i],
            logs.at[i],
            spread.at[i],
            dkv.at[k, pl.ds(0, GROUP)],
            dkv.at[k, pl.ds(GROUP, GROUP)],
            dq.at[i],
        )

    if dq_last:
        for i in range(2):
            dq_out[i] = (dq[i].T * 0.125).astype(dq_out.dtype)
    if dkv_last:
        dkv_out[...] = dkv[...].astype(dkv_out.dtype)


SLOW = 10**10
MIX = SLOW
JOIN = SLOW
JOIN_KEYS = 1 * 10**9
FORWARD = 0
PAIR = SLOW
WEIGHTS = 0
TILE_FLOPS = 2 * 10 * GROUP * GROUP * 64


def attention(order, name, qdo, kv, dq, dkv, dq_last=None, dkv_last=None, first=0, count=2):
    carry = [a for a in (dq, dkv) if a is not None]
    dq_shape = (2, LANES, GROUP) if dq_last is None else (2, GROUP, LANES)
    aliases = {}
    if dq is not None and dq_last is None:
        aliases[2] = 0
    if dkv is not None and dkv_last is None:
        aliases[1 + len(carry)] = 1
    return order.call(
        functools.partial(
            attention_kernel,
            first,
            count,
            dq is not None,
            dkv is not None,
            dq_last is not None,
            dkv_last is not None,
        ),
        [shaped(dq_shape, dq_last or F32), shaped((2, KV_ROWS, LANES), dkv_last or F32)],
        qdo,
        kv,
        *carry,
        scratch=[
            pltpu.VMEM((2, LANES, GROUP), BF16),
            pltpu.VMEM((2, 2, GROUP, LANES), BF16),
            pltpu.VMEM((2, 2, GROUP, LANES), BF16),
            pltpu.VMEM((2, 2, GROUP), F32),
            pltpu.VMEM((2, 2, GROUP), F32),
            pltpu.VMEM((2, LANES, GROUP), F32),
            pltpu.VMEM((2, KV_ROWS, LANES), F32),
        ],
        aliases=aliases,
        flops=2 * count * TILE_FLOPS,
        name="attention_" + name,
    )


def half_sum_kernel(totals, received, out):
    out[...] = (totals[1].astype(F32) + received[1].astype(F32)).astype(BF16)


def back_kernel(dq, dq_far, dq_near, dkv, dkv_far, dkv_near, keep, near, through, far):
    dq_sum = (dq[0] + dq_far[0].astype(F32) + dq_near[...].astype(F32)).astype(BF16)
    dkv_sum = (dkv[0] + dkv_far[0].astype(F32) + dkv_near[...].astype(F32)).astype(BF16)
    for j, (pay, base) in enumerate(((keep, 0), (near, 0), (through, 0), (far, 0))):
        pay[base : base + 128] = dq_sum[j * 128 : (j + 1) * 128]
        pay[base + 128 : base + 256] = dkv_sum[j * 128 : (j + 1) * 128]
        pay[base + 256 : base + 384] = dkv_sum[GROUP + j * 128 : GROUP + (j + 1) * 128]


def place_kernel(own, near, far, dq, dk, dv):
    me = place_in_group()
    for j, (pay, base) in enumerate(((own, 0), (near, 0), (far, 0), (far, 384))):
        columns = pl.ds(pl.multiple_of((me ^ j) * LANES, LANES), LANES)
        dq[:, columns] = pay[base : base + 128]
        dk[:, columns] = pay[base + 128 : base + 256]
        dv[:, columns] = pay[base + 256 : base + 384]


def turn_kernel(dq, out):
    for i in range(2):
        out[i] = dq[i].T * 0.125


def weights_kernel(source_ref, count_ref, tiles, grad, mix_ref, own, partner, near, crossed, far, keep_ref, send_ref, window, total, left_ref):
    core = lax.axis_index("c")
    window[REACH] = own[...]
    window[jnp.where(core == 0, 4, 2)] = partner[...]
    for block, first in ((near, jnp.where(core == 0, 1, 4)), (crossed, jnp.where(core == 0, 5, 0))):
        window[first] = block[0:128]
        window[first + 1] = block[128:256]
    window[6 * core] = far[...]
    total[...] = jnp.zeros_like(total)
    for e in range(tiles.shape[1]):

        @pl.when(e < count_ref[0])
        def _():
            total[...] += dot(tiles[0, e], window[slot_of(source_ref, e)], NN)

    left_ref[0] = turned(mix_ref[...])
    left_ref[1] = turned(total[...].astype(BF16))

    for out, which in ((keep_ref, core), (send_ref, 1 - core)):
        out[...] = dot(left_ref[which], grad[...], NN).astype(BF16)


def block_rows(distance):
    return pl.ds(pl.multiple_of(lax.rem(ring_place() + distance, 4) * 128, 128), 128)


def core_sum_kernel(keep, received, *outs):
    for k, out in enumerate(outs):
        rows = block_rows(k)
        out[...] = (keep[rows].astype(F32) + received[rows].astype(F32)).astype(out.dtype)


def gather_kernel(*refs):
    for k, block in enumerate(refs[:4]):
        refs[4][block_rows((4 - k) % 4)] = block[...]


def final_kernel(own, other, first, second):
    core = lax.axis_index("c")

    @pl.when(core == 0)
    def _():
        first[...] = own[...].astype(F32)
        second[...] = other[...].astype(F32)

    @pl.when(core == 1)
    def _():
        first[...] = other[...].astype(F32)
        second[...] = own[...].astype(F32)


def add_kernel(*refs):
    total = refs[0][...].astype(F32)
    for ref in refs[1:-1]:
        total = total + ref[...].astype(F32)
    refs[-1][...] = total.astype(BF16)


def add(order, name, *terms):
    (out,) = order.call(add_kernel, [shaped(terms[0].shape)], *terms, name="add_" + name)
    return out


def pair(order, first, second):
    (out,) = order.call(pair_kernel, [shaped((2,) + first.shape)], first, second, flops=PAIR, name="pair")
    return out


def body(
    features,
    queries,
    keys,
    values,
    attn_mix,
    log_sums,
    out_weight,
    msg_weight,
    edge_tiles,
    edge_source,
    edge_count,
    out_grad,
):
    rows, columns = out_grad.shape
    order = Order()
    other_grad = swap(out_grad, "h", 1)
    parts = lax.axis_size(NODE)
    to_near = [(i, (i + (2 if i % 2 == 0 else -2)) % parts) for i in range(parts)]
    to_far = [(i, (i + (-3 if i % 2 == 0 else 3)) % parts) for i in range(parts)]
    partner_features = swap(features, "c", 1)
    far_features = lax.ppermute(features, NODE, to_far)
    arguments = [features, edge_tiles, out_grad, queries, keys, values, log_sums, out_weight, attn_mix, msg_weight]
    arguments = [pltpu.with_memory_space_constraint(a, pltpu.HBM) for a in arguments]
    loaded = order.call(
        functools.partial(load_kernel, len(arguments)),
        [shaped(a.shape, a.dtype) for a in arguments],
        *arguments,
        anywhere=len(arguments),
        scratch=[pltpu.SemaphoreType.DMA((len(arguments),))],
        name="load",
    )
    features, edge_tiles, out_grad, queries, keys, values, log_sums, out_weight, attn_mix, msg_weight = loaded
    wide = (rows, 2 * columns)
    key_pays = order.call(
        pay_kernel, [shaped((KV_PAY, LANES))] * 4, keys, values, name="pay"
    )
    key_near, key_cross = swap(key_pays[1], "c", 1), swap(key_pays[3], "c", 1)
    (near_features,) = order.call(
        chip_kernel, [shaped((2 * rows, columns))], features, partner_features, name="chip"
    )
    near_features = lax.ppermute(near_features, NODE, to_near)
    (key_far,) = order.call(
        forward_kernel, [shaped((2 * KV_PAY, LANES))], key_pays[2], key_cross, name="forward_keys"
    )
    key_far = swap(key_far, "y", 1)
    out_grad, *pays = order.call(
        mix_kernel,
        [shaped(wide)] + [shaped((Q_PAY, LANES))] * 4,
        out_grad,
        other_grad,
        out_weight,
        attn_mix,
        queries,
        log_sums,
        flops=MIX,
        name="mix",
    )
    pay_near, pay_cross = swap(pays[1], "c", 1), swap(pays[3], "c", 1)
    (pay_far,) = order.call(
        forward_kernel, [shaped((2 * Q_PAY, LANES))], pays[2], pay_cross, flops=FORWARD, name="forward"
    )
    pay_far = swap(pay_far, "y", 1)
    (kv,) = order.call(
        join_keys_kernel,
        [shaped((KV_ROWS, LANES))],
        key_pays[0],
        key_near,
        key_far,
        flops=JOIN_KEYS,
        name="join_keys",
    )
    kv_met = meet(kv, "x", 0)
    (qdo,) = order.call(
        join_rows_kernel,
        [shaped((Q_ROWS, LANES))],
        pays[0],
        pay_near,
        pay_far,
        flops=JOIN,
        name="join",
    )
    qdo_met = meet(qdo, "z", 0)
    crossed_features = swap(near_features, "c", 1)
    keep, send = order.call(
        weights_kernel,
        [shaped((columns, 2 * columns)), shaped((columns, 2 * columns))],
        edge_source,
        edge_count,
        edge_tiles,
        out_grad,
        attn_mix,
        features,
        partner_features,
        near_features,
        crossed_features,
        far_features,
        smem=2,
        scratch=[
            pltpu.VMEM((2 * REACH + 1, rows, columns), BF16),
            pltpu.VMEM((rows, columns), F32),
            pltpu.VMEM((2, columns, rows), BF16),
        ],
        flops=WEIGHTS,
        name="weights",
    )
    received = swap(send, "c", 1)
    kv_near = pair(order, kv, kv_met)
    kv_far = meet(kv_near, "x", 1)
    qdo_near = pair(order, qdo, qdo_met)
    qdo_far = meet(qdo_near, "z", 1)
    blocks = order.call(
        core_sum_kernel,
        [shaped(wide, F32)] + [shaped(wide)] * 3,
        keep,
        received,
        name="core_sum",
    )
    blocks = [blocks[0]] + [around(blocks[k], k) for k in range(1, 4)]
    share_send, share_far, share_keep, share_local = order.call(
        share_kernel,
        [
            shaped((3 * rows, columns)),
            shaped((rows, columns)),
            shaped((2 * rows, columns), F32),
            shaped((rows, columns), F32),
        ],
        edge_source,
        edge_count,
        edge_tiles,
        out_grad,
        msg_weight,
        smem=2,
        scratch=[pltpu.VMEM((2 * REACH + 1, rows, columns), F32)],
        name="shares",
    )
    share_received = swap(share_send, "c", 1)
    dq_near, dkv_near = attention(order, "near", qdo_near, kv_near, None, None)
    share_near, share_local = order.call(
        near_kernel,
        [shaped((2 * rows, columns)), shaped((rows, columns), F32)],
        share_keep,
        share_local,
        share_received,
        name="near",
    )
    share_far, share_near = lax.ppermute(share_far, NODE, to_far), lax.ppermute(share_near, NODE, to_near)
    dq_far, dkv_far = attention(order, "far", qdo_far, kv_far, None, None)
    part = add(order, "ring", *blocks)
    received = across(part, 0)
    share_cross, share_local = order.call(
        cross_kernel,
        [shaped((rows, columns)), shaped((rows, columns), F32)],
        share_local,
        share_near,
        share_far,
        flops=SLOW,
        name="cross",
    )
    share_cross = swap(share_cross, "c", 1)
    dq_near, dkv_far = attention(
        order, "far_keys0", qdo_near, kv_far, dq_near, dkv_far, first=0, count=1
    )
    part = add(order, "across0", part, received)
    received = across(part, 1)
    dq_near, dkv_far = attention(
        order, "far_keys1", qdo_near, kv_far, dq_near, dkv_far, None, BF16, first=1, count=1
    )
    dkv_met = meet(dkv_far, "x", 1)
    dq_far, dkv_near = attention(
        order, "far_queries0", qdo_far, kv_near, dq_far, dkv_near, first=0, count=1
    )
    part = add(order, "across1", part, received)
    received = swap(part, "y", 1)
    dq_far, dkv_near = attention(
        order, "far_queries1", qdo_far, kv_near, dq_far, dkv_near, BF16, F32, first=1, count=1
    )
    dq_met = meet(dq_far, "z", 1)
    part = add(order, "y", part, received)
    blocks = [part] + [around(part, k) for k in range(1, 4)]
    (half,) = order.call(
        half_sum_kernel, [shaped((KV_ROWS, LANES))], dkv_near, dkv_met, name="half_dkv"
    )
    dkv_last = meet(half, "x", 0)
    (dq_near,) = order.call(
        turn_kernel, [shaped((2, GROUP, LANES), F32)], dq_near, name="turn"
    )
    (half,) = order.call(half_sum_kernel, [shaped((GROUP, LANES))], dq_near, dq_met, name="half_dq")
    dq_last = meet(half, "z", 0)
    back_own, back_near, back_through, back_cross = order.call(
        back_kernel,
        [shaped((384, LANES))] * 4,
        dq_near,
        dq_met,
        dq_last,
        dkv_near,
        dkv_met,
        dkv_last,
        name="back",
    )
    back_near, back_cross = swap(back_near, "c", 1), swap(back_cross, "c", 1)
    (back_forward,) = order.call(
        forward_kernel, [shaped((768, LANES))], back_through, back_cross, name="forward_back"
    )
    back_far = swap(back_forward, "y", 1)
    (whole,) = order.call(gather_kernel, [shaped((columns, 2 * columns))], *blocks, name="gather")
    received = swap(whole, "c", 1)
    grad_features = add(order, "shares", share_local, share_cross)
    out_weight_grad, msg_weight_grad = order.call(
        final_kernel,
        [shaped((columns, 2 * columns), F32)] * 2,
        whole,
        received,
        name="final",
    )
    grad_query, grad_key, grad_value = order.call(
        place_kernel, [shaped((rows, columns))] * 3, back_own, back_near, back_far, name="place"
    )
    return (grad_features, grad_query, grad_key, grad_value, out_weight_grad, msg_weight_grad)


def solution(mesh):
    fine = Mesh(mesh.devices.reshape(4, 2, 4, 2, 2), NODE + ("h",))
    both = P(NODE, "h")
    placed = (
        both,
        both,
        both,
        both,
        both,
        P("h", NODE),
        P("h", None),
        P("h", None),
        P(NODE, None, None, None),
        P(NODE, None),
        P(NODE),
        both,
    )
    return jax.shard_map(
        body,
        mesh=fine,
        in_specs=placed,
        out_specs=(both, both, both, both, P("h", None), P("h", None)),
        check_vma=False,
    )
```
